128 devices in a mesh: fsdp: 128 (over y, x, z, core).
Axes of the slice: x: 4, y: 4, z: 4, core: 2. Of those that a mesh axis runs over, the one named last changes fastest.
Arguments:
- tokens: bfloat16 [256, 256, 768], P('fsdp'), may hold values from -6 to 6
- condition: bfloat16 [256, 768], P('fsdp'), may hold values from -6 to 6
- cotangent: bfloat16 [256, 256, 768], P('fsdp'), may hold values from -6 to 6
- ada_weight: bfloat16 [3538944], P('fsdp'), may hold values from -0.21875 to 0.21875
- ada_bias: bfloat16 [4608], P('fsdp'), may hold values from -3 to 3
- qkv_weight: bfloat16 [1769472], P('fsdp'), may hold values from -0.21875 to 0.21875
- qv_bias: bfloat16 [1536], P('fsdp'), may hold values from -2 to 2
- proj_weight: bfloat16 [589824], P('fsdp'), may hold values from -0.625 to 0.625
- proj_bias: bfloat16 [768], P('fsdp'), may hold values from -2 to 2
- fc1_weight: bfloat16 [2359296], P('fsdp'), may hold values from -0.21875 to 0.21875
- fc1_bias: bfloat16 [3072], P('fsdp'), may hold values from -2 to 2
- fc2_weight: bfloat16 [2359296], P('fsdp'), may hold values from -0.109375 to 0.109375
- fc2_bias: bfloat16 [768], P('fsdp'), may hold values from -2 to 2
Outputs:
- layer_out: bfloat16 [256, 256, 768], P('fsdp')
- tokens_grad: bfloat16 [256, 256, 768], P('fsdp')
- condition_grad: bfloat16 [256, 768], P('fsdp')
- ada_weight_grad: float32 [3538944], P('fsdp')
- ada_bias_grad: float32 [4608], P('fsdp')
- qkv_weight_grad: float32 [1769472], P('fsdp')
- qv_bias_grad: float32 [1536], P('fsdp')
- proj_weight_grad: float32 [589824], P('fsdp')
- proj_bias_grad: float32 [768], P('fsdp')
- fc1_weight_grad: float32 [2359296], P('fsdp')
- fc1_bias_grad: float32 [3072], P('fsdp')
- fc2_weight_grad: float32 [2359296], P('fsdp')
- fc2_bias_grad: float32 [768], P('fsdp')
The draws below stay inside these ranges and needn't reach their ends.
All inputs are finite; a program needn't handle non-finite values.
Results may differ from the reference program's by a relative error of at most 0.013.
The reference program's roundings to bfloat16 on the way count: a program that leaves them out, or rounds other values in their place, can miss the bound.
Values may be sent and summed in bfloat16 or wider, within the bound.
No kernel may reach another device: no remote copies, remote signals or barrier semaphores. Data moves between devices by JAX's collectives and lax.ppermute only.
A program may use at most 192 MiB of HBM per device.

```python
import math
import jax
import jax.numpy as jnp
from jax import lax

HEADS = 12
HEAD_DIM = 64
D = 768
FF = 3072
TOK = 256
SEQS = 256


def block_scale(key, dims, cuts, low, largest):
    def one(dim, parts):
        heights = jax.random.uniform(jax.random.fold_in(jax.random.fold_in(key, 6), dim), (parts,), jnp.float32, low / len(cuts), largest / len(cuts))
        return jnp.repeat(jnp.exp(heights), dims[dim] // parts).reshape((-1,) + (1,) * (len(dims) - dim - 1))

    gain = one(*cuts[0])
    for cut in cuts[1:]:
        gain = gain * one(*cut)
    return gain


def bell_draw(rng, extent, spread, reach, shards=(), held_as=jnp.bfloat16):
    level = block_scale(rng, extent, shards, -0.22, 0.18) if shards else 1.0
    values = jax.random.normal(rng, extent, jnp.float32) * spread * level
    return jnp.minimum(jnp.maximum(values, -reach), reach).astype(held_as)


def setup_inputs(seed: int = 0) -> dict:
    arg_keys = jax.random.split(jax.random.key(seed), 14)
    tokens = bell_draw(arg_keys[0], (SEQS, TOK, D), 1.0, 6.0, ((0, 128),))
    condition = bell_draw(arg_keys[1], (SEQS, D), 1.0, 6.0, ((0, 128),))
    cotangent = bell_draw(arg_keys[2], (SEQS, TOK, D), 1.0, 6.0, ((0, 128),))
    ada_weight = bell_draw(arg_keys[3], (6 * D * D,), D ** -0.5, 0.21875, ((0, 128),))
    ada_bias = bell_draw(arg_keys[4], (6 * D,), 0.5, 3.0, ((0, 128),))
    qkv_weight = bell_draw(arg_keys[5], (3 * D * D,), D ** -0.5, 0.21875, ((0, 128),))
    qv_bias = bell_draw(arg_keys[6], (2 * D,), 0.3, 2.0, ((0, 128),))
    proj_weight = bell_draw(arg_keys[7], (D * D,), (D // 8) ** -0.5, 0.625, ((0, 128),))
    proj_bias = bell_draw(arg_keys[8], (D,), 0.3, 2.0, ((0, 128),))
    fc1_weight = bell_draw(arg_keys[9], (D * FF,), D ** -0.5, 0.21875, ((0, 128),))
    fc1_bias = bell_draw(arg_keys[10], (FF,), 0.3, 2.0, ((0, 128),))
    fc2_weight = bell_draw(arg_keys[11], (FF * D,), FF ** -0.5, 0.109375, ((0, 128),))
    fc2_bias = bell_draw(arg_keys[12], (D,), 0.3, 2.0, ((0, 128),))
    return {"tokens": tokens, "condition": condition, "cotangent": cotangent, "ada_weight": ada_weight, "ada_bias": ada_bias, "qkv_weight": qkv_weight, "qv_bias": qv_bias, "proj_weight": proj_weight, "proj_bias": proj_bias, "fc1_weight": fc1_weight, "fc1_bias": fc1_bias, "fc2_weight": fc2_weight, "fc2_bias": fc2_bias}


HIGHEST_PRECISION = lax.Precision.HIGHEST
EPSILON = 1e-06

@jax.custom_vjp
def low(v):
    return lax.optimization_barrier(v.astype(jnp.bfloat16)).astype(jnp.float32)

@jax.custom_vjp
def low_back(v):
    return v

def low_keep(v):
    return (low(v), None)

def low_pass(kept, grad):
    return (grad,)

def back_keep(v):
    return (v, None)

def back_low(kept, grad):
    return (low(grad),)
low.defvjp(low_keep, low_pass)
low_back.defvjp(back_keep, back_low)

def normalize(values):
    centered = values - lax.optimization_barrier(jnp.mean(values, axis=-1, keepdims=True))
    return centered * lax.rsqrt(lax.optimization_barrier(jnp.mean(centered * centered, axis=-1, keepdims=True)) + EPSILON)

def reference(tokens, condition, cotangent, ada_weight, ada_bias, qkv_weight, qv_bias, proj_weight, proj_bias, fc1_weight, fc1_bias, fc2_weight, fc2_bias):
    group_size = math.gcd(SEQS, 16)
    blocks = SEQS // group_size
    scale_factor = HEAD_DIM ** (-0.5)

    def forward(inputs, conds, ada_mat, ada_vec, query_key_value_weight, qv_vec, projection_weight, projection_bias, up_projection_weight, up_projection_bias, down_projection_weight, down_vec):
        bias_full = jnp.concatenate([qv_vec[:D], jnp.zeros((D,), jnp.float32), qv_vec[D:]])

        def layer_block(block_pair):
            latents, embedding = block_pair
            modulation = low_back(jnp.dot(low(jax.nn.silu(embedding)), ada_mat, precision=HIGHEST_PRECISION) + ada_vec)
            portions = [segment[:, None, :] for segment in jnp.split(modulation, 6, axis=-1)]
            shift_attn, scale_attn, gate_attn, shift_mlp, scale_mlp, gate_mlp = portions
            residual_after_attention = low(normalize(latents) * (1.0 + scale_attn) + shift_attn)
            packed = low_back(low(jnp.einsum('gld,de->gle', residual_after_attention, query_key_value_weight, precision=HIGHEST_PRECISION) + bias_full))
            queries = packed[..., :D].reshape(group_size, TOK, HEADS, HEAD_DIM)
            keys_all = packed[..., D:2 * D].reshape(group_size, TOK, HEADS, HEAD_DIM)
            values_all = packed[..., 2 * D:].reshape(group_size, TOK, HEADS, HEAD_DIM)
            scores = low_back(jnp.einsum('gqhd,gkhd->ghqk', queries, keys_all, precision=HIGHEST_PRECISION) * scale_factor)
            probs = low(jax.nn.softmax(scores, axis=-1))
            modulated_normed = low_back(low(jnp.einsum('ghqk,gkhd->gqhd', probs, values_all, precision=HIGHEST_PRECISION).reshape(group_size, TOK, D)))
            attended = low_back(jnp.einsum('gld,de->gle', modulated_normed, projection_weight, precision=HIGHEST_PRECISION) + projection_bias)
            middle = latents + gate_attn * attended
            residual_after_feedforward = low(normalize(middle) * (1.0 + scale_mlp) + shift_mlp)
            expanded = low_back(jnp.einsum('gld,df->glf', residual_after_feedforward, up_projection_weight, precision=HIGHEST_PRECISION) + up_projection_bias)
            activated = low(jax.nn.gelu(expanded, approximate=True))
            branch = low_back(jnp.einsum('glf,fd->gld', activated, down_projection_weight, precision=HIGHEST_PRECISION) + down_vec)
            return middle + gate_mlp * branch
        outputs = lax.map(jax.checkpoint(layer_block), (inputs.reshape(blocks, group_size, TOK, D), conds.reshape(blocks, group_size, D)))
        return outputs.reshape(SEQS, TOK, D)
    result, backward = jax.vjp(forward, tokens.astype(jnp.float32), condition.astype(jnp.float32), ada_weight.astype(jnp.float32).reshape(D, 6 * D), ada_bias.astype(jnp.float32), qkv_weight.astype(jnp.float32).reshape(D, 3 * D), qv_bias.astype(jnp.float32), proj_weight.astype(jnp.float32).reshape(D, D), proj_bias.astype(jnp.float32), fc1_weight.astype(jnp.float32).reshape(D, FF), fc1_bias.astype(jnp.float32), fc2_weight.astype(jnp.float32).reshape(FF, D), fc2_bias.astype(jnp.float32))
    grads = backward(cotangent.astype(jnp.float32))
    return (result.astype(jnp.bfloat16), grads[0].astype(jnp.bfloat16), grads[1].astype(jnp.bfloat16), grads[2].reshape(-1), grads[3], grads[4].reshape(-1), grads[5], grads[6].reshape(-1), grads[7], grads[8].reshape(-1), grads[9], grads[10].reshape(-1), grads[11])
```

```python
from functools import partial

import jax
import jax.numpy as jnp
import numpy as np
from jax import lax
from jax.experimental import pallas as pl
from jax.experimental.pallas import tpu as pltpu
from jax.sharding import Mesh, PartitionSpec as P

HEADS = 12
HEAD_DIM = 64
D = 768
FF = 3072


EPSILON = 1e-06


def normalize(values):
    centered = values - jnp.mean(values, axis=-1, keepdims=True)
    inverse = lax.rsqrt(jnp.mean(centered * centered, axis=-1, keepdims=True) + EPSILON)
    return (centered * inverse, inverse)


def norm_back(grad_normed, normed, inverse):
    return inverse * (
        grad_normed
        - jnp.mean(grad_normed, axis=-1, keepdims=True)
        - normed * jnp.mean(grad_normed * normed, axis=-1, keepdims=True)
    )


DEVICES = 128
ROWS_ONE = 400
AXES = ("y", "x", "z", "c")
COLUMN = ("z", "c")
PLANE = ("y", "x")


def place(device):
    return device // 32, device // 8 % 4, device // 2 % 4, device % 2


def device_at(y, x, z, c):
    return ((y % 4 * 4 + x % 4) * 4 + z % 4) * 2 + c


def moved(kind, step):
    pairs = []
    for device in range(DEVICES):
        y, x, z, c = place(device)
        if kind == "core":
            target = device_at(y, x, z, 1 - c)
        elif kind == "z":
            target = device_at(y, x, z + step, c)
        elif (kind == "first") == (c == 0):
            target = device_at(y, x + step, z, c)
        else:
            target = device_at(y + step, x, z, c)
        pairs.append((device, target))
    return pairs


def send(values, kind, step=0):
    return lax.ppermute(values, AXES, moved(kind, step))


def plane_block(core, first, second):
    first, second = first % 4, second % 4
    return second * 4 + first if core == 0 else first * 4 + second


def table_row(device):
    y, x, z, core = place(device)
    first, second = (x, y) if core == 0 else (y, x)
    gather_steps = [(s, k) for s in (0, 1, -1, 2) for k in range(4)]
    row = np.zeros((104,), np.int32)
    row[0:5] = (core, z, 4 * y + x, z, core)
    row[8:24] = [plane_block(core, first - k, second - s) for s, k in gather_steps]
    row[24:40] = [plane_block(1 - core, second - k, first - s) for s, k in gather_steps]
    row[40:42] = (core, 1 - core)
    row[48:64] = [
        plane_block(core, first + k, second + s) for s in (2, 1, -1, 0) for k in range(4)
    ]
    row[64] = core
    for i in range(16):
        up, across = i // 4, i % 4
        row[72 + i] = plane_block(core, x - across, y - up) if core == 0 else plane_block(0, y - up, x - across)
        row[88 + i] = plane_block(0, across - x, up - y) if core == 0 else plane_block(0, up - y, across - x)
    return row


TABLE = np.stack([table_row(device) for device in range(DEVICES)])


def gathered(values, kind):
    return jnp.stack([values] + [send(values, kind, k) for k in (1, 2, 3)])


def collect_column(where, mine, theirs, held, sems):
    z, core = where[0], where[1]
    copies = []
    for k in range(4):
        spot = 2 * ((z + 4 - k) % 4)
        copies.append(pltpu.make_async_copy(mine.at[k], held.at[spot + core], sems.at[0, k]))
        copies.append(pltpu.make_async_copy(theirs.at[k], held.at[spot + 1 - core], sems.at[1, k]))
    for copy in copies:
        copy.start()
    for copy in copies:
        copy.wait()


def spread(held, flat, start, used, padded):
    for j in range(8):
        flat[j * used : (j + 1) * used, :] = held[j, start : start + padded, :].astype(jnp.float32)[
            :used
        ]


def relayout_one_kernel(where, mine, theirs, payload, ada, bias, held, flat, sems):
    collect_column(where, mine, theirs, held, sems)
    core = where[1]
    spread(held, flat, 0, 108, 112)
    for k in range(9):
        payload[:, 128 * k : 128 * k + 128] = flat[pl.ds(9 * core + k, 48, stride=18), :].astype(
            jnp.bfloat16
        )
    spread(held, flat, 112, 36, 48)
    for k in range(3):
        payload[:, 1152 + 128 * k : 1280 + 128 * k] = flat[
            pl.ds(3 * core + k, 48, stride=6), :
        ].astype(jnp.bfloat16)
    spread(held, flat, 160, 216, 224)
    for k in range(36):
        ada[:, 128 * k : 128 * k + 128] = flat[pl.ds(k, 48, stride=36), :].astype(jnp.bfloat16)
    bias[...] = held[:, 384:400, :].astype(jnp.float32)


def relayout_two_kernel(where, held, payload, flat):
    spread(held, flat, 0, 144, 144)
    for k in range(24):
        payload[:, 128 * k : 128 * k + 128] = flat[pl.ds(k, 48, stride=24), :].astype(
            jnp.bfloat16
        )
    spread(held, flat, 144, 144, 144)
    for q in range(4):
        for k in range(6):
            lane = FF + D * q + 128 * k
            payload[:, lane : lane + 128] = flat[
                pl.ds(288 * q + k, 48, stride=6), :
            ].astype(jnp.bfloat16)


def pack_kernel(*refs):
    out, rows = refs[-2:]
    for j in range(6):
        for s in range(2):
            rows[6 * s + j : 6 * s + j + 1, :] = refs[j][s : s + 1, :]
    start = 12
    for ref in refs[6:10]:
        rows[start : start + ref.shape[0], :] = ref[...]
        start += ref.shape[0]
    rows[start:, :] = jnp.zeros((24 - start, D), jnp.float32)
    out[...] = rows[...].astype(jnp.bfloat16)


ANYWHERE = pl.BlockSpec(memory_space=pl.ANY)
SCALARS = pl.BlockSpec(memory_space=pltpu.SMEM)
LIMIT = pltpu.CompilerParams(vmem_limit_bytes=40 * 1024 * 1024)


VMEM = pl.BlockSpec(memory_space=pltpu.VMEM)


def relayout_two(where, held):
    return pl.pallas_call(
        relayout_two_kernel,
        out_shape=jax.ShapeDtypeStruct((48, 2 * FF), jnp.bfloat16),
        in_specs=[SCALARS, VMEM],
        out_specs=VMEM,
        scratch_shapes=[pltpu.VMEM((1152, 128), jnp.float32)],
        compiler_params=LIMIT,
    )(where, held)


def relayout(kernel, rows, flat_rows, outs, where, mine, theirs):
    return pl.pallas_call(
        kernel,
        out_shape=outs,
        in_specs=[SCALARS, ANYWHERE, ANYWHERE],
        out_specs=[VMEM] * 3,
        scratch_shapes=[
            pltpu.VMEM((8, rows, 128), jnp.bfloat16),
            pltpu.VMEM((flat_rows, 128), jnp.float32),
            pltpu.SemaphoreType.DMA((2, 4)),
        ],
        compiler_params=LIMIT,
    )(where, mine, theirs)


def assemble(kernel, outs, spots, mine, theirs):
    return pl.pallas_call(
        kernel,
        out_shape=outs,
        in_specs=[SCALARS] + [ANYWHERE] * 10,
        out_specs=[pl.BlockSpec(memory_space=pltpu.VMEM)] * 2,
        scratch_shapes=[pltpu.SemaphoreType.DMA((2, 16, 5))],
        compiler_params=LIMIT,
    )(spots, *mine, *theirs)


def sources(groups):
    return [(group, k) for group, count in zip(groups, (4, 4, 4, 2, 2)) for k in range(count)]


def assemble_one_kernel(spots, *refs):
    qkv, proj, sems = refs[10:]
    copies = []
    for side in range(2):
        core = spots[32 + side]
        for i, (group, k) in enumerate(sources(refs[5 * side : 5 * side + 5])):
            rows = pl.ds(pl.multiple_of(48 * spots[16 * side + i], 48), 48)
            copies.append(
                pltpu.make_async_copy(
                    group.at[k, :, 0:1152],
                    qkv.at[rows, pl.ds(pl.multiple_of(1152 * core, 128), 1152)],
                    sems.at[side, i, 0],
                )
            )
            copies.append(
                pltpu.make_async_copy(
                    group.at[k, :, 1152:1536],
                    proj.at[rows, pl.ds(pl.multiple_of(384 * core, 128), 384)],
                    sems.at[side, i, 1],
                )
            )
    for copy in copies:
        copy.start()
    for copy in copies:
        copy.wait()


def ring_gather(payload):
    base = gathered(payload, "first")
    low = send(base, "second", 1)
    high = send(base, "second", -1)
    far_low = send(low[:2], "second", 1)
    far_high = send(high[2:], "second", -1)
    mine = [base, low, high, far_low, far_high]
    return mine, [send(group, "core") for group in mine]


def sum_one_kernel(spots, qkv, qkv_in, out):
    total = qkv[...].astype(jnp.float32) + qkv_in[...].astype(jnp.float32)
    out[0] = total.astype(jnp.bfloat16)


def wide(values):
    return values.astype(jnp.float32)


def ring_sum(blocks):
    far, high, low_, base = blocks[0:4], blocks[4:8], blocks[8:12], blocks[12:16]
    far_low = send(far[:2], "second", 1)
    far_high = send(far[2:], "second", -1)
    high = jnp.concatenate([(wide(high[:2]) + wide(far_low)).astype(jnp.bfloat16), high[2:]])
    low_ = jnp.concatenate([low_[:2], (wide(low_[2:]) + wide(far_high)).astype(jnp.bfloat16)])
    from_low = send(high, "second", 1)
    from_high = send(low_, "second", -1)
    base = wide(base) + wide(from_low) + wide(from_high)
    total = base[0]
    for k in (1, 2, 3):
        total = total + wide(send(base[k].astype(jnp.bfloat16), "first", k))
    return total


def column_sum(rows, z):
    parts = rows.reshape(4, 12, -1)
    parts = lax.dynamic_slice_in_dim(jnp.concatenate([parts, parts]), z, 4, axis=0)
    total = parts[0]
    for k in (1, 2, 3):
        total = total + wide(send(parts[k].astype(jnp.bfloat16), "z", k))
    return total.reshape(2, 6, -1)


def other_half(values, core):
    half = values.shape[-1] // 2
    return jnp.where(core == 0, values[:, half:], values[:, :half])


def own_half(values, core):
    half = values.shape[-1] // 2
    return jnp.where(core == 0, values[:, :half], values[:, half:])


def joined(mine, received, core):
    return jnp.where(
        core == 0,
        jnp.concatenate([mine, received], axis=-1),
        jnp.concatenate([received, mine], axis=-1),
    ).reshape(-1)


def total_of(values):
    return jnp.sum(values, axis=(0, 1), dtype=jnp.float32)


def body(
    tokens,
    condition,
    cotangent,
    ada_weight,
    ada_bias,
    qkv_weight,
    qv_bias,
    proj_weight,
    proj_bias,
    fc1_weight,
    fc1_bias,
    fc2_weight,
    fc2_bias,
):
    table = lax.dynamic_index_in_dim(
        jnp.asarray(TABLE), lax.axis_index(AXES), axis=0, keepdims=False
    )
    core, z, plane_index = table[0], table[1], table[2]
    where = table[3:5]
    spots = table[8:42]
    sum_spots = table[48:65]
    reverse_spots = table[72:88]
    order = table[88:104]
    def padded(values, rows):
        values = values.reshape(-1, 128)
        return jnp.concatenate([values, jnp.zeros((rows - values.shape[0], 128), jnp.bfloat16)])

    bias_row = jnp.zeros((128,), jnp.bfloat16)
    start = 0
    for bias in (qv_bias, proj_bias, fc1_bias, fc2_bias, ada_bias):
        stop = start + bias.shape[0]
        bias_row = bias_row + jnp.pad(bias, (start, 128 - stop))
        start = stop
    own_one = jnp.concatenate(
        [
            padded(qkv_weight, 112),
            padded(proj_weight, 48),
            padded(ada_weight, 224),
            padded(bias_row, 16),
        ]
    )
    own_two = jnp.concatenate([fc1_weight.reshape(-1, 128), fc2_weight.reshape(-1, 128)])
    column_two = lax.all_gather(own_two, COLUMN, axis=0, tiled=True).reshape(8, 288, 128)
    weights_two = lax.all_gather(relayout_two(where, column_two), PLANE, axis=0, tiled=True)
    up_projection_weight = weights_two[:, :FF]
    down_projection_weight = (
        weights_two[:, FF:].reshape(16, 48, 4, D).transpose(0, 2, 1, 3).reshape(FF, D)
    )
    column_one = gathered(own_one, "z")
    plane_small = gathered(gathered(padded(condition, 16), "first"), "second").reshape(16, 16, 128)
    column_one_in = send(column_one, "core")
    payload_one, ada_rows, bias_block = relayout(
        relayout_one_kernel,
        ROWS_ONE,
        1728,
        [
            jax.ShapeDtypeStruct((48, 1536), jnp.bfloat16),
            jax.ShapeDtypeStruct((48, 6 * D), jnp.bfloat16),
            jax.ShapeDtypeStruct((8, 16, 128), jnp.float32),
        ],
        where,
        column_one,
        column_one_in,
    )
    mine_one, theirs_one = ring_gather(payload_one)
    embed_plane = plane_small[:, :12].reshape(32, D)
    embed_plane_low = jax.nn.silu(embed_plane.astype(jnp.float32)).astype(jnp.bfloat16)
    embed_rows = lax.dynamic_slice(embed_plane_low, (0, 48 * plane_index), (32, 48))
    bias_block = bias_block[:, 0, :]
    ada_bias_row = lax.dynamic_update_slice(
        jnp.zeros((6 * D,), jnp.float32), bias_block[:, 48:84].reshape(-1), (288 * plane_index,)
    )
    bias_slots = lax.dynamic_update_slice(
        jnp.zeros((16, 384), jnp.float32),
        bias_block[:, 0:48].reshape(1, 384),
        (plane_index, 0),
    )
    modulation_part = jnp.concatenate(
        [
            jnp.dot(embed_rows, ada_rows, preferred_element_type=jnp.float32) + ada_bias_row,
            jnp.broadcast_to(bias_slots.reshape(1, 2, 4 * D), (16, 2, 4 * D)).reshape(32, 4 * D),
        ],
        axis=1,
    ).reshape(4, 8, 10 * D)
    modulation_rows = modulation_part[0]
    for k in (1, 2, 3):
        modulation_rows = modulation_rows + send(modulation_part[k], "second", -k)
    modulation_rows = modulation_rows.reshape(4, 2, 10 * D)
    modulation = modulation_rows[0]
    for k in (1, 2, 3):
        modulation = modulation + send(modulation_rows[k], "first", -k)
    bias_rows = modulation[:, 6 * D :].reshape(16, 8, 48)
    modulation = modulation[:, : 6 * D]
    qv_vec = bias_rows[:, :, 0:12].reshape(-1)
    projection_bias = bias_rows[:, :, 12:18].reshape(-1)
    up_projection_bias = bias_rows[:, :, 18:42].reshape(-1)
    down_vec = bias_rows[:, :, 42:48].reshape(-1)
    query_key_value_weight, projection_weight = assemble(
        assemble_one_kernel,
        [
            jax.ShapeDtypeStruct((D, 3 * D), jnp.bfloat16),
            jax.ShapeDtypeStruct((D, D), jnp.bfloat16),
        ],
        spots,
        mine_one,
        theirs_one,
    )
    seqs_here = tokens.shape[0]
    length = tokens.shape[1]
    scale_factor = HEAD_DIM ** (-0.5)
    latents = tokens.astype(jnp.float32)
    embedding = condition.astype(jnp.float32)
    _, silu_back = jax.vjp(jax.nn.silu, embedding)
    portions = [segment[:, None, :] for segment in jnp.split(modulation, 6, axis=-1)]
    shift_attn, scale_attn, gate_attn, shift_mlp, scale_mlp, gate_mlp = portions
    normed_one, inverse_one = normalize(latents)
    residual_after_attention = (normed_one * (1.0 + scale_attn) + shift_attn).astype(jnp.bfloat16)
    bias_full = jnp.concatenate([qv_vec[:D], jnp.zeros((D,), jnp.float32), qv_vec[D:]])
    packed = (
        jnp.einsum(
            "obc,cg->obg",
            residual_after_attention,
            query_key_value_weight,
            preferred_element_type=jnp.float32,
        )
        + bias_full
    ).astype(jnp.bfloat16)
    queries = packed[..., :D].reshape(seqs_here, length, HEADS, HEAD_DIM)
    keys_all = packed[..., D : 2 * D].reshape(seqs_here, length, HEADS, HEAD_DIM)
    values_all = packed[..., 2 * D :].reshape(seqs_here, length, HEADS, HEAD_DIM)
    scores = (
        jnp.einsum("sqhd,skhd->shqk", queries, keys_all, preferred_element_type=jnp.float32)
        * scale_factor
    )
    log_total = jax.nn.logsumexp(scores, axis=-1, keepdims=True)
    probs_low = jnp.exp(scores - log_total).astype(jnp.bfloat16)
    modulated_normed = (
        jnp.einsum("shqk,skhd->sqhd", probs_low, values_all, preferred_element_type=jnp.float32)
        .reshape(seqs_here, length, D)
        .astype(jnp.bfloat16)
    )
    attended = (
        jnp.einsum(
            "obc,cg->obg", modulated_normed, projection_weight, preferred_element_type=jnp.float32
        )
        + projection_bias
    )
    middle = latents + gate_attn * attended
    normed_two, inverse_two = normalize(middle)
    residual_after_feedforward = (normed_two * (1.0 + scale_mlp) + shift_mlp).astype(jnp.bfloat16)
    expanded = (
        jnp.einsum(
            "eob,br->eor",
            residual_after_feedforward,
            up_projection_weight,
            preferred_element_type=jnp.float32,
        )
        + up_projection_bias
    )
    activated, gelu_back = jax.vjp(partial(jax.nn.gelu, approximate=True), expanded)
    activated_reduced = activated.astype(jnp.bfloat16)
    branch = (
        jnp.einsum(
            "bth,ha->bta",
            activated_reduced,
            down_projection_weight,
            preferred_element_type=jnp.float32,
        )
        + down_vec
    )
    result = middle + gate_mlp * branch
    grad_out = cotangent.astype(jnp.float32)
    residual_branch_gradient = (gate_mlp * grad_out).astype(jnp.bfloat16)
    gate_mlp_grad = jnp.sum(grad_out * branch, axis=1)
    down_grad = jnp.einsum(
        "igm,igu->mu",
        activated_reduced,
        residual_branch_gradient,
        preferred_element_type=jnp.float32,
    )
    down_bias_grad = total_of(residual_branch_gradient)
    activated_grad = jnp.einsum(
        "zoh,vh->zov",
        residual_branch_gradient,
        down_projection_weight,
        preferred_element_type=jnp.float32,
    )
    expanded_hidden_gradient = gelu_back(activated_grad)[0].astype(jnp.bfloat16)
    up_grad = jnp.einsum(
        "gck,gci->ki",
        residual_after_feedforward,
        expanded_hidden_gradient,
        preferred_element_type=jnp.float32,
    )
    up_bias_grad = total_of(expanded_hidden_gradient)
    hidden_two_grad = jnp.einsum(
        "mwh,oh->mwo",
        expanded_hidden_gradient,
        up_projection_weight,
        preferred_element_type=jnp.float32,
    )
    shift_mlp_grad = jnp.sum(hidden_two_grad, axis=1)
    scale_mlp_grad = jnp.sum(hidden_two_grad * normed_two, axis=1)
    middle_grad = grad_out + norm_back(hidden_two_grad * (1.0 + scale_mlp), normed_two, inverse_two)
    attention_output_gradient = (gate_attn * middle_grad).astype(jnp.bfloat16)
    gate_attn_grad = jnp.sum(middle_grad * attended, axis=1)
    projection_gradient = jnp.einsum(
        "jxc,jxh->ch",
        modulated_normed,
        attention_output_gradient,
        preferred_element_type=jnp.float32,
    )
    proj_bias_grad = total_of(attention_output_gradient)
    summand_two = jnp.concatenate(
        [
            up_grad.astype(jnp.bfloat16),
            down_grad.astype(jnp.bfloat16)
            .reshape(16, 4, 48, D)
            .transpose(0, 2, 1, 3)
            .reshape(D, FF),
            projection_gradient.astype(jnp.bfloat16),
        ],
        axis=1,
    )
    attention_output_gradient, summand_two = lax.optimization_barrier(
        (attention_output_gradient, summand_two)
    )
    rows_two = wide(lax.psum_scatter(summand_two, PLANE, scatter_dimension=0, tiled=True))
    mixed_grad = (
        jnp.einsum(
            "ohz,kz->ohk",
            attention_output_gradient,
            projection_weight,
            preferred_element_type=jnp.float32,
        )
        .astype(jnp.bfloat16)
        .reshape(seqs_here, length, HEADS, HEAD_DIM)
    )
    scores_again = (
        jnp.einsum("sqhd,skhd->shqk", queries, keys_all, preferred_element_type=jnp.float32)
        * scale_factor
    )
    probs = jnp.exp(scores_again - log_total)
    probs_again = probs.astype(jnp.bfloat16)
    values_grad = jnp.einsum(
        "shqk,sqhd->skhd", probs_again, mixed_grad, preferred_element_type=jnp.float32
    )
    probs_grad = jnp.einsum(
        "sqhd,skhd->shqk", mixed_grad, values_all, preferred_element_type=jnp.float32
    )
    scores_grad = (
        probs * (probs_grad - jnp.sum(probs_grad * probs, axis=-1, keepdims=True))
    ).astype(jnp.bfloat16)
    queries_grad = (
        jnp.einsum("shqk,skhd->sqhd", scores_grad, keys_all, preferred_element_type=jnp.float32)
        * scale_factor
    )
    keys_grad = (
        jnp.einsum("shqk,sqhd->skhd", scores_grad, queries, preferred_element_type=jnp.float32)
        * scale_factor
    )
    packed_query_key_value_gradient = jnp.concatenate(
        [
            queries_grad.reshape(seqs_here, length, D),
            keys_grad.reshape(seqs_here, length, D),
            values_grad.reshape(seqs_here, length, D),
        ],
        axis=-1,
    ).astype(jnp.bfloat16)
    qkv_grad = jnp.einsum(
        "jxc,jxh->ch",
        residual_after_attention,
        packed_query_key_value_gradient,
        preferred_element_type=jnp.float32,
    )
    qv_bias_grad = jnp.concatenate(
        [
            total_of(packed_query_key_value_gradient[..., :D]),
            total_of(packed_query_key_value_gradient[..., 2 * D :]),
        ]
    )
    hidden_one_grad = jnp.einsum(
        "ohz,kz->ohk",
        packed_query_key_value_gradient,
        query_key_value_weight,
        preferred_element_type=jnp.float32,
    )
    shift_attn_grad = jnp.sum(hidden_one_grad, axis=1)
    scale_attn_grad = jnp.sum(hidden_one_grad * normed_one, axis=1)
    input_grad = middle_grad + norm_back(
        hidden_one_grad * (1.0 + scale_attn), normed_one, inverse_one
    )
    packed_small = pl.pallas_call(
        pack_kernel,
        out_shape=jax.ShapeDtypeStruct((24, D), jnp.bfloat16),
        in_specs=[VMEM] * 10,
        out_specs=VMEM,
        scratch_shapes=[pltpu.VMEM((24, D), jnp.float32)],
    )(
        shift_attn_grad,
        scale_attn_grad,
        gate_attn_grad,
        shift_mlp_grad,
        scale_mlp_grad,
        gate_mlp_grad,
        qv_bias_grad.reshape(2, D),
        proj_bias_grad.reshape(1, D),
        up_bias_grad.reshape(4, D),
        down_bias_grad.reshape(1, D),
    )
    plane_grads = gathered(gathered(packed_small, "first"), "second").reshape(16, 24, D)
    modulation_grads = plane_grads[:, :12].reshape(32, 6 * D)
    bias_sums = jnp.sum(plane_grads[:, 12:20], axis=0, dtype=jnp.float32).reshape(-1)
    ada_grad = jnp.einsum(
        "sd,se->de", embed_rows, modulation_grads, preferred_element_type=jnp.float32
    )
    ada_bias_sums = jnp.sum(modulation_grads, axis=0, dtype=jnp.float32)
    embed_part = jnp.einsum(
        "se,de->sd", modulation_grads, ada_rows, preferred_element_type=jnp.float32
    ).reshape(4, 8, 48)
    embed_rows_in = jnp.stack(
        [embed_part[0]] + [send(embed_part[k], "second", -k) for k in (1, 2, 3)]
    ).reshape(4, 4, 2, 48)
    embed_parts = jnp.stack(
        [embed_rows_in[:, 0]] + [send(embed_rows_in[:, k], "first", -k) for k in (1, 2, 3)],
        axis=1,
    ).reshape(16, 2, 48)
    embed_sum = jnp.take(embed_parts, order, axis=0).transpose(1, 0, 2).reshape(2, D)
    embed_grad = silu_back(embed_sum)[0]

    qkv_grad = qkv_grad.astype(jnp.bfloat16)
    blocks_one = pl.pallas_call(
        sum_one_kernel,
        grid_spec=pltpu.PrefetchScalarGridSpec(
            num_scalar_prefetch=1,
            grid=(16,),
            in_specs=[
                pl.BlockSpec((48, 1152), lambda i, spots: (spots[i], spots[16])),
                pl.BlockSpec((48, 1152), lambda i, spots: (spots[i], 0)),
            ],
            out_specs=pl.BlockSpec((1, 48, 1152), lambda i, spots: (i, 0, 0)),
        ),
        out_shape=jax.ShapeDtypeStruct((16, 48, 1152), jnp.bfloat16),
        compiler_params=LIMIT,
    )(sum_spots, qkv_grad, send(other_half(qkv_grad, core), "core"))
    rows_one = ring_sum(blocks_one)
    bias_parts = []
    start = 0
    for size in (12, 6, 24, 6):
        bias_parts.append(
            lax.dynamic_slice(
                bias_sums[start : start + 128 * size], (8 * size * plane_index,), (8 * size,)
            ).reshape(8, size)
        )
        start += 128 * size
    bias_parts.append(
        lax.dynamic_slice(ada_bias_sums, (288 * plane_index,), (288,)).reshape(8, 36)
    )
    bias_block = jnp.pad(
        jnp.concatenate(bias_parts, axis=1).reshape(48, 14), ((0, 0), (0, 128 - 14))
    )
    down_rows = rows_two[:, FF : 2 * FF].reshape(48, 4, D).transpose(1, 0, 2).reshape(48, FF)
    wide_rows = jnp.concatenate(
        [ada_grad, rows_two[:, :FF], down_rows, rows_two[:, 2 * FF :]], axis=-1
    )
    pieces = []
    start = 0
    for width in (6 * D, FF, D, D, D, D, D):
        pieces.append(wide_rows[:, start : start + width])
        start += width
    out_half = jnp.concatenate([other_half(piece, core) for piece in pieces] + [bias_block], axis=-1)
    own = jnp.concatenate([own_half(piece, core) for piece in pieces] + [bias_block], axis=-1)
    own = own + wide(send(out_half.astype(jnp.bfloat16), "core"))
    rows_all = column_sum(jnp.concatenate([rows_one, own], axis=-1), z)
    mine = jnp.where(core == 0, rows_all[0], rows_all[1])
    received = wide(
        send(
            jnp.where(core == 0, rows_all[1], rows_all[0])[:, :6912].astype(jnp.bfloat16),
            "core",
        )
    )

    def cut(start, width, groups=1):
        return joined(
            mine[:, start : start + width].reshape(6, groups, -1),
            received[:, start : start + width].reshape(6, groups, -1),
            core,
        )

    bias_shard = mine[:, 6912:6926].reshape(-1)
    return (
        result.astype(jnp.bfloat16),
        input_grad.astype(jnp.bfloat16),
        embed_grad.astype(jnp.bfloat16),
        cut(1152, 2304),
        bias_shard[48:84],
        cut(0, 1152),
        bias_shard[0:12],
        cut(6528, 384),
        bias_shard[12:18],
        cut(3456, 1536),
        bias_shard[18:42],
        cut(4992, 1536, 4),
        bias_shard[42:48],
    )


def solution(mesh):
    return jax.shard_map(
        body,
        mesh=Mesh(mesh.devices.reshape(4, 4, 4, 2), AXES),
        in_specs=(
            P(AXES, None, None),
            P(AXES, None),
            P(AXES, None, None),
            P(AXES),
            P(AXES),
            P(AXES),
            P(AXES),
            P(AXES),
            P(AXES),
            P(AXES),
            P(AXES),
            P(AXES),
            P(AXES),
        ),
        out_specs=(
            P(AXES, None, None),
            P(AXES, None, None),
            P(AXES, None),
            P(AXES),
            P(AXES),
            P(AXES),
            P(AXES),
            P(AXES),
            P(AXES),
            P(AXES),
            P(AXES),
            P(AXES),
            P(AXES),
        ),
        check_vma=False,
    )
```

```python
import jax
import jax.numpy as jnp
import numpy as np
from jax import lax
from jax.experimental import pallas as pl
from jax.experimental.pallas import tpu as pltpu
from jax.sharding import Mesh, PartitionSpec as P

HEADS = 12
HEAD_DIM = 64
D = 768
FF = 3072


TOK = 256
EPSILON = 1e-06
SCALE = HEAD_DIM ** (-0.5)
GELU = (2.0 / np.pi) ** 0.5


DEVICES = 128
ROWS_ONE = 688
AXES = ("y", "x", "z", "c")
COLUMN = ("z", "c")
PLANE = ("y", "x")


def place(device):
    return device // 32, device // 8 % 4, device // 2 % 4, device % 2


def device_at(y, x, z, c):
    return ((y % 4 * 4 + x % 4) * 4 + z % 4) * 2 + c


def moved(kind, step):
    pairs = []
    for device in range(DEVICES):
        y, x, z, c = place(device)
        if kind == "core":
            target = device_at(y, x, z, 1 - c)
        elif kind == "z":
            target = device_at(y, x, z + step, c)
        elif (kind == "first") == (c == 0):
            target = device_at(y, x + step, z, c)
        else:
            target = device_at(y + step, x, z, c)
        pairs.append((device, target))
    return pairs


def send(values, kind, step=0):
    return lax.ppermute(values, AXES, moved(kind, step))


def plane_block(core, first, second):
    first, second = first % 4, second % 4
    return second * 4 + first if core == 0 else first * 4 + second


def table_row(device):
    y, x, z, core = place(device)
    first, second = (x, y) if core == 0 else (y, x)
    gather_steps = [(s, k) for s in (0, 1, -1, 2) for k in range(4)]
    row = np.zeros((104,), np.int32)
    row[0:5] = (core, z, 4 * y + x, z, core)
    row[8:24] = [plane_block(core, first - k, second - s) for s, k in gather_steps]
    row[24:40] = [plane_block(1 - core, second - k, first - s) for s, k in gather_steps]
    row[40:42] = (core, 1 - core)
    row[48:64] = [
        plane_block(core, first + k, second + s) for s in (2, 1, -1, 0) for k in range(4)
    ]
    row[64] = core
    for i in range(16):
        up, across = i // 4, i % 4
        row[72 + i] = plane_block(core, x - across, y - up) if core == 0 else plane_block(0, y - up, x - across)
        row[88 + i] = plane_block(0, across - x, up - y) if core == 0 else plane_block(0, up - y, across - x)
    return row


TABLE = np.stack([table_row(device) for device in range(DEVICES)])


def gathered(values, kind):
    return jnp.stack([values] + [send(values, kind, k) for k in (1, 2, 3)])


def collect_column(where, mine, theirs, held, sems):
    z, core = where[0], where[1]
    copies = []
    for k in range(4):
        spot = 2 * ((z + 4 - k) % 4)
        copies.append(pltpu.make_async_copy(mine.at[k], held.at[spot + core], sems.at[0, k]))
        copies.append(pltpu.make_async_copy(theirs.at[k], held.at[spot + 1 - core], sems.at[1, k]))
    for copy in copies:
        copy.start()
    for copy in copies:
        copy.wait()


def spread(held, flat, start, used, padded):
    for j in range(8):
        flat[j * used : (j + 1) * used, :] = held[j, start : start + padded, :].astype(jnp.float32)[
            :used
        ]


def relayout_one_kernel(where, mine, theirs, payload, ada, bias, payload_two, held, flat, sems):
    collect_column(where, mine, theirs, held, sems)
    core = where[1]
    spread(held, flat, 0, 108, 112)
    for k in range(9):
        payload[:, 128 * k : 128 * k + 128] = flat[pl.ds(9 * core + k, 48, stride=18), :].astype(
            jnp.bfloat16
        )
    spread(held, flat, 112, 36, 48)
    for k in range(3):
        payload[:, 1152 + 128 * k : 1280 + 128 * k] = flat[
            pl.ds(3 * core + k, 48, stride=6), :
        ].astype(jnp.bfloat16)
    spread(held, flat, 160, 216, 224)
    for k in range(36):
        ada[:, 128 * k : 128 * k + 128] = flat[pl.ds(k, 48, stride=36), :].astype(jnp.bfloat16)
    bias[...] = held[:, 384:400, :].astype(jnp.float32)
    relayout_two(held, payload_two, flat)


def relayout_two(held, payload, flat):
    spread(held, flat, 400, 144, 144)
    for k in range(24):
        payload[:, 128 * k : 128 * k + 128] = flat[pl.ds(k, 48, stride=24), :].astype(
            jnp.bfloat16
        )
    spread(held, flat, 544, 144, 144)
    for q in range(4):
        for k in range(6):
            lane = FF + D * q + 128 * k
            payload[:, lane : lane + 128] = flat[
                pl.ds(288 * q + k, 48, stride=6), :
            ].astype(jnp.bfloat16)


def pack_kernel(*refs):
    out, rows = refs[-2:]
    for j in range(6):
        for s in range(2):
            rows[6 * s + j : 6 * s + j + 1, :] = refs[j][s : s + 1, :]
    start = 12
    for ref in refs[6:10]:
        rows[start : start + ref.shape[0], :] = ref[...]
        start += ref.shape[0]
    rows[start:, :] = jnp.zeros((24 - start, D), jnp.float32)
    out[...] = rows[...].astype(jnp.bfloat16)


ANYWHERE = pl.BlockSpec(memory_space=pl.ANY)
SCALARS = pl.BlockSpec(memory_space=pltpu.SMEM)
LIMIT = pltpu.CompilerParams(vmem_limit_bytes=56 * 1024 * 1024)


VMEM = pl.BlockSpec(memory_space=pltpu.VMEM)


def relayout(kernel, rows, flat_rows, outs, where, mine, theirs):
    return pl.pallas_call(
        kernel,
        out_shape=outs,
        in_specs=[SCALARS, ANYWHERE, ANYWHERE],
        out_specs=[VMEM] * 4,
        scratch_shapes=[
            pltpu.VMEM((8, rows, 128), jnp.bfloat16),
            pltpu.VMEM((flat_rows, 128), jnp.float32),
            pltpu.SemaphoreType.DMA((2, 4)),
        ],
        compiler_params=LIMIT,
    )(where, mine, theirs)


def sources(groups):
    return [(group, k) for group, count in zip(groups, (4, 4, 4, 2, 2)) for k in range(count)]


def place_weights(spots, groups, qkv, proj, sems):
    copies = []
    for side in range(2):
        core = spots[32 + side]
        for i, (group, k) in enumerate(sources(groups[5 * side : 5 * side + 5])):
            rows = pl.ds(pl.multiple_of(48 * spots[16 * side + i], 16), 48)
            copies.append(
                pltpu.make_async_copy(
                    group.at[k, :, 0:1152],
                    qkv.at[rows, pl.ds(pl.multiple_of(1152 * core, 128), 1152)],
                    sems.at[side, i, 0],
                )
            )
            copies.append(
                pltpu.make_async_copy(
                    group.at[k, :, 1152:1536],
                    proj.at[rows, pl.ds(pl.multiple_of(384 * core, 128), 384)],
                    sems.at[side, i, 1],
                )
            )
    return copies


def dot(left, right, contract=(1, 0)):
    return lax.dot_general(
        left,
        right,
        (((contract[0],), (contract[1],)), ((), ())),
        preferred_element_type=jnp.float32,
    )


def low(values):
    return values.astype(jnp.bfloat16)


def normalize(values):
    centered = values - jnp.mean(values, axis=-1, keepdims=True)
    inverse = lax.rsqrt(jnp.mean(centered * centered, axis=-1, keepdims=True) + EPSILON)
    return centered * inverse, inverse


def norm_back(grad, normed, inverse):
    return inverse * (
        grad
        - jnp.mean(grad, axis=-1, keepdims=True)
        - normed * jnp.mean(grad * normed, axis=-1, keepdims=True)
    )


def part(modulation, s, j):
    return modulation[s : s + 1, D * j : D * j + D]


def lane_halves():
    lane = lax.broadcasted_iota(jnp.int32, (TOK, 128), 1)
    return lane < 64, lane >= 64


def probabilities(query, key):
    scores = dot(query, key, (1, 1)) * SCALE
    weights = jnp.exp(scores - jnp.max(scores, axis=-1, keepdims=True))
    return weights * (1.0 / jnp.sum(weights, axis=-1, keepdims=True))


def attention_kernel(spots, x, modulation, qkv_bias, proj_bias, *refs):
    groups, (h1, packed, mixed, attended, middle, h2, qkv, proj, sems) = refs[:10], refs[10:]
    copies = place_weights(spots, groups, qkv, proj, sems)
    for copy in copies:
        copy.start()
    for s in range(2):
        rows = slice(TOK * s, TOK * s + TOK)
        normed, _ = normalize(wide(x[rows]))
        h1[rows] = low(normed * (1.0 + part(modulation, s, 1)) + part(modulation, s, 0))
    for copy in copies:
        copy.wait()
    first_half, _ = lane_halves()
    zero = jnp.zeros((TOK, 128), jnp.bfloat16)
    for s in range(2):
        rows = slice(TOK * s, TOK * s + TOK)
        for t in range(3):
            lanes = slice(D * t, D * t + D)
            packed[rows, lanes] = low(dot(h1[rows], qkv[:, lanes]) + qkv_bias[:, lanes])
        for pair in range(6):
            query = packed[rows, 128 * pair : 128 * pair + 128]
            key = packed[rows, D + 128 * pair : D + 128 * pair + 128]
            value = packed[rows, 2 * D + 128 * pair : 2 * D + 128 * pair + 128]
            one = dot(low(probabilities(jnp.where(first_half, query, zero), key)), value)
            two = dot(low(probabilities(jnp.where(first_half, zero, query), key)), value)
            mixed[rows, 128 * pair : 128 * pair + 128] = low(jnp.where(first_half, one, two))
        branch = dot(mixed[rows], proj[...]) + proj_bias[...]
        attended[rows] = branch
        after = wide(x[rows]) + part(modulation, s, 2) * branch
        middle[rows] = after
        normed, _ = normalize(after)
        h2[rows] = low(normed * (1.0 + part(modulation, s, 4)) + part(modulation, s, 3))


def total(values):
    return jnp.sum(values, axis=0, keepdims=True)


def mlp_kernel(
    middle, attended, h2, mixed, cotangent, modulation, up_bias, down_bias, weights,
    result, middle_grad, branch_grad, summand,
    gate_one, shift_two, scale_two, gate_two, proj_sum, down_sum, up_sum,
    up, down, active, hidden_grad, out_grad, branch, hidden_two, sems,
):
    copies = [pltpu.make_async_copy(weights.at[:, 0:FF], up, sems.at[64])]
    for b in range(16):
        for q in range(4):
            start = 192 * b + 48 * q
            copies.append(
                pltpu.make_async_copy(
                    weights.at[48 * b : 48 * b + 48, FF + D * q : FF + D * q + D],
                    down.at[start : start + 48, :],
                    sems.at[4 * b + q],
                )
            )
    for copy in copies:
        copy.start()
    for s in range(2):
        rows = slice(TOK * s, TOK * s + TOK)
        out_grad[rows] = low(part(modulation, s, 5) * wide(cotangent[rows]))
    for copy in copies:
        copy.wait()
    for s in range(2):
        rows = slice(TOK * s, TOK * s + TOK)
        for t in range(6):
            lanes = slice(512 * t, 512 * t + 512)
            value = dot(h2[rows], up[:, lanes]) + up_bias[:, lanes]
            square = value * value
            bend = jnp.tanh(GELU * (value + 0.044715 * (square * value)))
            active[rows, lanes] = low(0.5 * value * (1.0 + bend))
            slope = 0.5 * (1.0 + bend) + 0.5 * value * (1.0 - bend * bend) * (
                GELU * (1.0 + 3 * 0.044715 * square)
            )
            grad = low(dot(out_grad[rows], down[lanes, :], (1, 1)) * slope)
            hidden_grad[rows, lanes] = grad
            sums = total(wide(grad))
            if s == 0:
                up_sum[:, lanes] = sums
            else:
                up_sum[:, lanes] = up_sum[:, lanes] + sums
        branch[...] = dot(active[rows], down[...]) + down_bias[...]
        hidden_two[...] = dot(hidden_grad[rows], up[...], (1, 1))
        given = wide(cotangent[rows])
        after = middle[rows]
        result[rows] = low(after + part(modulation, s, 5) * branch[...])
        gate_two[s : s + 1] = total(given * branch[...])
        normed, inverse = normalize(after)
        grad = hidden_two[...]
        shift_two[s : s + 1] = total(grad)
        scale_two[s : s + 1] = total(grad * normed)
        grad = given + norm_back(grad * (1.0 + part(modulation, s, 4)), normed, inverse)
        middle_grad[rows] = grad
        gate_one[s : s + 1] = total(grad * attended[rows])
        branch_grad[rows] = low(part(modulation, s, 2) * grad)
    proj_sum[...] = total(wide(branch_grad[...]))
    down_sum[...] = total(wide(out_grad[...]))
    for t in range(4):
        lanes = slice(D * t, D * t + D)
        summand[:, lanes] = low(dot(h2[...], hidden_grad[:, lanes], (0, 0)))
    for t in range(8):
        tile = low(dot(active[:, 384 * t : 384 * t + 384], out_grad[...], (0, 0)))
        for j in range(8):
            b, q = 2 * t + j // 4, j % 4
            summand[48 * b : 48 * b + 48, FF + D * q : FF + D * q + D] = tile[
                48 * j : 48 * j + 48
            ]
    summand[:, 2 * FF :] = low(dot(mixed[...], branch_grad[...], (0, 0)))


def attention_back_kernel(
    where, x, modulation, packed, h1, branch_grad, middle_grad, qkv, proj,
    tokens_grad, mine, theirs, shift_one, scale_one, qv_sum,
    mixed_grad, packed_grad,
):
    first_half, _ = lane_halves()
    zero = jnp.zeros((TOK, 128), jnp.bfloat16)
    for s in range(2):
        rows = slice(TOK * s, TOK * s + TOK)
        mixed_grad[...] = low(dot(branch_grad[rows], proj[...], (1, 1)))
        for pair in range(6):
            lanes = slice(128 * pair, 128 * pair + 128)
            query = packed[rows, lanes]
            key = packed[rows, D + 128 * pair : D + 128 * pair + 128]
            value = packed[rows, 2 * D + 128 * pair : 2 * D + 128 * pair + 128]
            grad = mixed_grad[:, lanes]
            query_grads = []
            key_grad = None
            for half in range(2):
                if half == 0:
                    own_query = jnp.where(first_half, query, zero)
                    own_grad = jnp.where(first_half, grad, zero)
                else:
                    own_query = jnp.where(first_half, zero, query)
                    own_grad = jnp.where(first_half, zero, grad)
                probs = probabilities(own_query, key)
                from_value = dot(low(probs), own_grad, (0, 0))
                probs_grad = dot(own_grad, value, (1, 1))
                scores_grad = low(
                    probs
                    * (probs_grad - jnp.sum(probs_grad * probs, axis=-1, keepdims=True))
                )
                query_grads.append(dot(scores_grad, key))
                from_key = dot(scores_grad, own_query, (0, 0))
                if key_grad is None:
                    key_grad, value_grad = from_key, from_value
                else:
                    key_grad, value_grad = key_grad + from_key, value_grad + from_value
            packed_grad[rows, lanes] = low(
                jnp.where(first_half, query_grads[0], query_grads[1]) * SCALE
            )
            packed_grad[rows, D + 128 * pair : D + 128 * pair + 128] = low(key_grad * SCALE)
            packed_grad[rows, 2 * D + 128 * pair : 2 * D + 128 * pair + 128] = low(value_grad)
        grad = dot(packed_grad[rows], qkv[...], (1, 1))
        normed, inverse = normalize(wide(x[rows]))
        shift_one[s : s + 1] = total(grad)
        scale_one[s : s + 1] = total(grad * normed)
        tokens_grad[rows] = low(
            middle_grad[rows] + norm_back(grad * (1.0 + part(modulation, s, 1)), normed, inverse)
        )
    qv_sum[0:1] = total(wide(packed_grad[:, 0:D]))
    qv_sum[1:2] = total(wide(packed_grad[:, 2 * D :]))
    for out, core in ((theirs, 1 - where[1]), (mine, where[1])):
        for t in range(3):
            lanes = pl.ds(pl.multiple_of(1152 * core + 384 * t, 128), 384)
            out[:, 384 * t : 384 * t + 384] = low(dot(h1[...], packed_grad[:, lanes], (0, 0)))


def shaped(*shape, dtype=jnp.float32):
    return jax.ShapeDtypeStruct(shape, dtype)


def cost(flops, moved):
    return pl.CostEstimate(flops=flops, bytes_accessed=moved, transcendentals=0)


def ring_gather(payload):
    base = gathered(payload, "first")
    low = send(base, "second", 1)
    high = send(base, "second", -1)
    far_low = send(low[:2], "second", 1)
    far_high = send(high[2:], "second", -1)
    mine = [base, low, high, far_low, far_high]
    return mine, [send(group, "core") for group in mine]


def sum_kernel(spots, mine, received, out):
    for i in range(16):
        rows = pl.ds(pl.multiple_of(48 * spots[i], 16), 48)
        out[i] = low(wide(mine[rows, :]) + wide(received[rows, :]))


def wide(values):
    return values.astype(jnp.float32)


def ring_sum(blocks):
    far, high, low_, base = blocks[0:4], blocks[4:8], blocks[8:12], blocks[12:16]
    far_low = send(far[:2], "second", 1)
    far_high = send(far[2:], "second", -1)
    high = jnp.concatenate([(wide(high[:2]) + wide(far_low)).astype(jnp.bfloat16), high[2:]])
    low_ = jnp.concatenate([low_[:2], (wide(low_[2:]) + wide(far_high)).astype(jnp.bfloat16)])
    from_low = send(high, "second", 1)
    from_high = send(low_, "second", -1)
    base = wide(base) + wide(from_low) + wide(from_high)
    total = base[0]
    for k in (1, 2, 3):
        total = total + wide(send(base[k].astype(jnp.bfloat16), "first", k))
    return total


def column_sum(rows, z):
    parts = rows.reshape(4, 12, -1)
    parts = lax.dynamic_slice_in_dim(jnp.concatenate([parts, parts]), z, 4, axis=0)
    total = parts[0]
    for k in (1, 2, 3):
        total = total + wide(send(parts[k].astype(jnp.bfloat16), "z", k))
    return total.reshape(2, 6, -1)


def other_half(values, core):
    half = values.shape[-1] // 2
    return jnp.where(core == 0, values[:, half:], values[:, :half])


def own_half(values, core):
    half = values.shape[-1] // 2
    return jnp.where(core == 0, values[:, :half], values[:, half:])


def joined(mine, received, core):
    return jnp.where(
        core == 0,
        jnp.concatenate([mine, received], axis=-1),
        jnp.concatenate([received, mine], axis=-1),
    ).reshape(-1)


def body(
    tokens,
    condition,
    cotangent,
    ada_weight,
    ada_bias,
    qkv_weight,
    qv_bias,
    proj_weight,
    proj_bias,
    fc1_weight,
    fc1_bias,
    fc2_weight,
    fc2_bias,
):
    table = lax.dynamic_index_in_dim(
        jnp.asarray(TABLE), lax.axis_index(AXES), axis=0, keepdims=False
    )
    core, z, plane_index = table[0], table[1], table[2]
    where = table[3:5]
    spots = table[8:42]
    sum_spots = table[48:65]
    reverse_spots = table[72:88]
    order = table[88:104]
    def padded(values, rows):
        values = values.reshape(-1, 128)
        return jnp.concatenate([values, jnp.zeros((rows - values.shape[0], 128), jnp.bfloat16)])

    bias_row = jnp.zeros((128,), jnp.bfloat16)
    start = 0
    for bias in (qv_bias, proj_bias, fc1_bias, fc2_bias, ada_bias):
        stop = start + bias.shape[0]
        bias_row = bias_row + jnp.pad(bias, (start, 128 - stop))
        start = stop
    own_one = jnp.concatenate(
        [
            padded(qkv_weight, 112),
            padded(proj_weight, 48),
            padded(ada_weight, 224),
            padded(bias_row, 16),
            fc1_weight.reshape(-1, 128),
            fc2_weight.reshape(-1, 128),
        ]
    )
    column_one = gathered(own_one, "z")
    plane_small = gathered(gathered(padded(condition, 16), "first"), "second").reshape(16, 16, 128)
    column_one_in = send(column_one, "core")
    payload_one, ada_rows, bias_block, payload_two = relayout(
        relayout_one_kernel,
        ROWS_ONE,
        1728,
        [
            jax.ShapeDtypeStruct((48, 1536), jnp.bfloat16),
            jax.ShapeDtypeStruct((48, 6 * D), jnp.bfloat16),
            jax.ShapeDtypeStruct((8, 16, 128), jnp.float32),
            jax.ShapeDtypeStruct((48, 2 * FF), jnp.bfloat16),
        ],
        where,
        column_one,
        column_one_in,
    )
    weights_two = lax.all_gather(payload_two, PLANE, axis=0, tiled=True)
    mine_one, theirs_one = ring_gather(payload_one)
    embed_plane = plane_small[:, :12].reshape(32, D)
    embed_plane_low = jax.nn.silu(embed_plane.astype(jnp.float32)).astype(jnp.bfloat16)
    embed_rows = lax.dynamic_slice(embed_plane_low, (0, 48 * plane_index), (32, 48))
    bias_block = bias_block[:, 0, :]
    ada_bias_row = lax.dynamic_update_slice(
        jnp.zeros((6 * D,), jnp.float32), bias_block[:, 48:84].reshape(-1), (288 * plane_index,)
    )
    bias_slots = lax.dynamic_update_slice(
        jnp.zeros((16, 384), jnp.float32),
        bias_block[:, 0:48].reshape(1, 384),
        (plane_index, 0),
    )
    modulation_part = jnp.concatenate(
        [
            jnp.dot(embed_rows, ada_rows, preferred_element_type=jnp.float32) + ada_bias_row,
            jnp.broadcast_to(bias_slots.reshape(1, 2, 4 * D), (16, 2, 4 * D)).reshape(32, 4 * D),
        ],
        axis=1,
    ).reshape(4, 8, 10 * D)
    modulation_rows = modulation_part[0]
    for k in (1, 2, 3):
        modulation_rows = modulation_rows + send(modulation_part[k], "second", -k)
    modulation_rows = modulation_rows.reshape(4, 2, 10 * D)
    modulation = modulation_rows[0]
    for k in (1, 2, 3):
        modulation = modulation + send(modulation_rows[k], "first", -k)
    bias_rows = modulation[:, 6 * D :].reshape(16, 8, 48)
    modulation = modulation[:, : 6 * D]
    qv_vec = bias_rows[:, :, 0:12].reshape(-1)
    projection_bias = bias_rows[:, :, 12:18].reshape(-1)
    up_projection_bias = bias_rows[:, :, 18:42].reshape(-1)
    down_vec = bias_rows[:, :, 42:48].reshape(-1)
    bias_full = jnp.concatenate([qv_vec[:D], jnp.zeros((D,), jnp.float32), qv_vec[D:]])
    latents = tokens.reshape(2 * TOK, D)
    h1, packed, mixed, attended, middle, h2, qkv_whole, proj_whole = pl.pallas_call(
        attention_kernel,
        out_shape=[
            shaped(512, D, dtype=jnp.bfloat16),
            shaped(512, 3 * D, dtype=jnp.bfloat16),
            shaped(512, D, dtype=jnp.bfloat16),
            shaped(512, D),
            shaped(512, D),
            shaped(512, D, dtype=jnp.bfloat16),
            shaped(D, 3 * D, dtype=jnp.bfloat16),
            shaped(D, D, dtype=jnp.bfloat16),
        ],
        in_specs=[SCALARS] + [VMEM] * 4 + [ANYWHERE] * 10,
        out_specs=[VMEM] * 8,
        scratch_shapes=[pltpu.SemaphoreType.DMA((2, 16, 2))],
        compiler_params=LIMIT,
        cost_estimate=cost(3 * 10**9, 2 * 10**7),
    )(
        spots,
        latents,
        modulation,
        bias_full.reshape(1, 3 * D),
        projection_bias.reshape(1, D),
        *mine_one,
        *theirs_one,
    )
    (
        result,
        middle_grad,
        branch_grad,
        summand_two,
        gate_attn_grad,
        shift_mlp_grad,
        scale_mlp_grad,
        gate_mlp_grad,
        proj_bias_grad,
        down_bias_grad,
        up_bias_grad,
    ) = pl.pallas_call(
        mlp_kernel,
        out_shape=[
            shaped(512, D, dtype=jnp.bfloat16),
            shaped(512, D),
            shaped(512, D, dtype=jnp.bfloat16),
            shaped(D, 9 * D, dtype=jnp.bfloat16),
            shaped(2, D),
            shaped(2, D),
            shaped(2, D),
            shaped(2, D),
            shaped(1, D),
            shaped(1, D),
            shaped(1, FF),
        ],
        in_specs=[VMEM] * 8 + [ANYWHERE],
        out_specs=[VMEM] * 11,
        scratch_shapes=[
            pltpu.VMEM((D, FF), jnp.bfloat16),
            pltpu.VMEM((FF, D), jnp.bfloat16),
            pltpu.VMEM((512, FF), jnp.bfloat16),
            pltpu.VMEM((512, FF), jnp.bfloat16),
            pltpu.VMEM((512, D), jnp.bfloat16),
            pltpu.VMEM((TOK, D), jnp.float32),
            pltpu.VMEM((TOK, D), jnp.float32),
            pltpu.SemaphoreType.DMA((65,)),
        ],
        compiler_params=LIMIT,
        cost_estimate=cost(15 * 10**9, 3 * 10**7),
    )(
        middle,
        attended,
        h2,
        mixed,
        cotangent.reshape(2 * TOK, D),
        modulation,
        up_projection_bias.reshape(1, FF),
        down_vec.reshape(1, D),
        weights_two,
    )
    branch_grad, summand_two = lax.optimization_barrier((branch_grad, summand_two))
    rows_two = wide(lax.psum_scatter(summand_two, PLANE, scatter_dimension=0, tiled=True))
    input_grad, grad_mine, grad_theirs, shift_attn_grad, scale_attn_grad, qv_bias_grad = (
        pl.pallas_call(
            attention_back_kernel,
            out_shape=[
                shaped(512, D, dtype=jnp.bfloat16),
                shaped(D, 1152, dtype=jnp.bfloat16),
                shaped(D, 1152, dtype=jnp.bfloat16),
                shaped(2, D),
                shaped(2, D),
                shaped(2, D),
            ],
            in_specs=[SCALARS] + [VMEM] * 8,
            out_specs=[VMEM] * 6,
            scratch_shapes=[
                pltpu.VMEM((TOK, D), jnp.bfloat16),
                pltpu.VMEM((512, 3 * D), jnp.bfloat16),
            ],
            compiler_params=LIMIT,
            cost_estimate=cost(8 * 10**9, 2 * 10**7),
        )(where, latents, modulation, packed, h1, branch_grad, middle_grad, qkv_whole, proj_whole)
    )
    packed_small = pl.pallas_call(
        pack_kernel,
        out_shape=jax.ShapeDtypeStruct((24, D), jnp.bfloat16),
        in_specs=[VMEM] * 10,
        out_specs=VMEM,
        scratch_shapes=[pltpu.VMEM((24, D), jnp.float32)],
    )(
        shift_attn_grad,
        scale_attn_grad,
        gate_attn_grad,
        shift_mlp_grad,
        scale_mlp_grad,
        gate_mlp_grad,
        qv_bias_grad,
        proj_bias_grad,
        up_bias_grad.reshape(4, D),
        down_bias_grad,
    )
    plane_grads = gathered(gathered(packed_small, "first"), "second").reshape(16, 24, D)
    modulation_grads = plane_grads[:, :12].reshape(32, 6 * D)
    bias_sums = jnp.sum(plane_grads[:, 12:20], axis=0, dtype=jnp.float32).reshape(-1)
    ada_grad = jnp.einsum(
        "sd,se->de", embed_rows, modulation_grads, preferred_element_type=jnp.float32
    )
    ada_bias_sums = jnp.sum(modulation_grads, axis=0, dtype=jnp.float32)
    embed_part = jnp.einsum(
        "se,de->sd", modulation_grads, ada_rows, preferred_element_type=jnp.float32
    ).reshape(4, 8, 48)
    embed_rows_in = jnp.stack(
        [embed_part[0]] + [send(embed_part[k], "second", -k) for k in (1, 2, 3)]
    ).reshape(4, 4, 2, 48)
    embed_parts = jnp.stack(
        [embed_rows_in[:, 0]] + [send(embed_rows_in[:, k], "first", -k) for k in (1, 2, 3)],
        axis=1,
    ).reshape(16, 2, 48)
    embed_sum = jnp.take(embed_parts, order, axis=0).transpose(1, 0, 2).reshape(2, D)
    _, silu_back = jax.vjp(jax.nn.silu, condition.astype(jnp.float32))
    embed_grad = silu_back(embed_sum)[0]

    blocks_one = pl.pallas_call(
        sum_kernel,
        out_shape=shaped(16, 48, 1152, dtype=jnp.bfloat16),
        in_specs=[SCALARS, VMEM, VMEM],
        out_specs=VMEM,
        compiler_params=LIMIT,
    )(sum_spots, grad_mine, send(grad_theirs, "core"))
    rows_one = ring_sum(blocks_one)
    bias_parts = []
    start = 0
    for size in (12, 6, 24, 6):
        bias_parts.append(
            lax.dynamic_slice(
                bias_sums[start : start + 128 * size], (8 * size * plane_index,), (8 * size,)
            ).reshape(8, size)
        )
        start += 128 * size
    bias_parts.append(
        lax.dynamic_slice(ada_bias_sums, (288 * plane_index,), (288,)).reshape(8, 36)
    )
    bias_block = jnp.pad(
        jnp.concatenate(bias_parts, axis=1).reshape(48, 14), ((0, 0), (0, 128 - 14))
    )
    down_rows = rows_two[:, FF : 2 * FF].reshape(48, 4, D).transpose(1, 0, 2).reshape(48, FF)
    wide_rows = jnp.concatenate(
        [ada_grad, rows_two[:, :FF], down_rows, rows_two[:, 2 * FF :]], axis=-1
    )
    pieces = []
    start = 0
    for width in (6 * D, FF, D, D, D, D, D):
        pieces.append(wide_rows[:, start : start + width])
        start += width
    out_half = jnp.concatenate([other_half(piece, core) for piece in pieces] + [bias_block], axis=-1)
    own = jnp.concatenate([own_half(piece, core) for piece in pieces] + [bias_block], axis=-1)
    own = own + wide(send(out_half.astype(jnp.bfloat16), "core"))
    rows_all = column_sum(jnp.concatenate([rows_one, own], axis=-1), z)
    mine = jnp.where(core == 0, rows_all[0], rows_all[1])
    received = wide(
        send(
            jnp.where(core == 0, rows_all[1], rows_all[0])[:, :6912].astype(jnp.bfloat16),
            "core",
        )
    )

    def cut(start, width, groups=1):
        return joined(
            mine[:, start : start + width].reshape(6, groups, -1),
            received[:, start : start + width].reshape(6, groups, -1),
            core,
        )

    bias_shard = mine[:, 6912:6926].reshape(-1)
    return (
        result.reshape(tokens.shape),
        input_grad.reshape(tokens.shape),
        embed_grad.astype(jnp.bfloat16),
        cut(1152, 2304),
        bias_shard[48:84],
        cut(0, 1152),
        bias_shard[0:12],
        cut(6528, 384),
        bias_shard[12:18],
        cut(3456, 1536),
        bias_shard[18:42],
        cut(4992, 1536, 4),
        bias_shard[42:48],
    )


def solution(mesh):
    return jax.shard_map(
        body,
        mesh=Mesh(mesh.devices.reshape(4, 4, 4, 2), AXES),
        in_specs=(
            P(AXES, None, None),
            P(AXES, None),
            P(AXES, None, None),
            P(AXES),
            P(AXES),
            P(AXES),
            P(AXES),
            P(AXES),
            P(AXES),
            P(AXES),
            P(AXES),
            P(AXES),
            P(AXES),
        ),
        out_specs=(
            P(AXES, None, None),
            P(AXES, None, None),
            P(AXES, None),
            P(AXES),
            P(AXES),
            P(AXES),
            P(AXES),
            P(AXES),
            P(AXES),
            P(AXES),
            P(AXES),
            P(AXES),
            P(AXES),
        ),
        check_vma=False,
    )
```

```python
import jax
import jax.numpy as jnp
import numpy as np
from jax import lax
from jax.experimental import pallas as pl
from jax.experimental.pallas import tpu as pltpu
from jax.sharding import Mesh, PartitionSpec as P

HEADS = 12
HEAD_DIM = 64
D = 768
FF = 3072


TOK = 256
EPSILON = 1e-06
SCALE = HEAD_DIM ** (-0.5)
GELU = (2.0 / np.pi) ** 0.5


DEVICES = 128
ROWS_ONE = 688
AXES = ("y", "x", "z", "c")
COLUMN = ("z", "c")
PLANE = ("y", "x")


def place(device):
    return device // 32, device // 8 % 4, device // 2 % 4, device % 2


def device_at(y, x, z, c):
    return ((y % 4 * 4 + x % 4) * 4 + z % 4) * 2 + c


def moved(kind, step):
    pairs = []
    for device in range(DEVICES):
        y, x, z, c = place(device)
        if kind == "core":
            target = device_at(y, x, z, 1 - c)
        elif kind == "z":
            target = device_at(y, x, z + step, c)
        elif (kind == "first") == (c == 0):
            target = device_at(y, x + step, z, c)
        else:
            target = device_at(y + step, x, z, c)
        pairs.append((device, target))
    return pairs


def send(values, kind, step=0):
    return lax.ppermute(values, AXES, moved(kind, step))


def plane_block(core, first, second):
    first, second = first % 4, second % 4
    return second * 4 + first if core == 0 else first * 4 + second


def table_row(device):
    y, x, z, core = place(device)
    first, second = (x, y) if core == 0 else (y, x)
    gather_steps = [(s, k) for s in (0, 1, -1, 2) for k in range(4)]
    row = np.zeros((104,), np.int32)
    row[0:5] = (core, z, 4 * y + x, z, core)
    row[8:24] = [plane_block(core, first - k, second - s) for s, k in gather_steps]
    row[24:40] = [plane_block(1 - core, second - k, first - s) for s, k in gather_steps]
    row[40:42] = (core, 1 - core)
    row[48:64] = [
        plane_block(core, first + k, second + s) for s in (2, 1, -1, 0) for k in range(4)
    ]
    row[64] = core
    for i in range(16):
        up, across = i // 4, i % 4
        row[72 + i] = plane_block(core, x - across, y - up) if core == 0 else plane_block(0, y - up, x - across)
        row[88 + i] = plane_block(0, across - x, up - y) if core == 0 else plane_block(0, up - y, across - x)
    return row


TABLE = np.stack([table_row(device) for device in range(DEVICES)])


def gathered(values, kind):
    return jnp.stack([values] + [send(values, kind, k) for k in (1, 2, 3)])


def collect_column(where, mine, theirs, held, sems):
    z, core = where[0], where[1]
    copies = []
    for k in range(4):
        spot = 2 * ((z + 4 - k) % 4)
        copies.append(pltpu.make_async_copy(mine.at[k], held.at[spot + core], sems.at[0, k]))
        copies.append(pltpu.make_async_copy(theirs.at[k], held.at[spot + 1 - core], sems.at[1, k]))
    for copy in copies:
        copy.start()
    for copy in copies:
        copy.wait()


def spread(held, flat, start, used, padded):
    for j in range(8):
        flat[j * used : (j + 1) * used, :] = held[j, start : start + padded, :].astype(jnp.float32)[
            :used
        ]


def relayout_one_kernel(where, mine, theirs, payload, ada, bias, payload_two, held, flat, sems):
    collect_column(where, mine, theirs, held, sems)
    core = where[1]
    spread(held, flat, 0, 108, 112)
    for k in range(9):
        payload[:, 128 * k : 128 * k + 128] = flat[pl.ds(9 * core + k, 48, stride=18), :].astype(
            jnp.bfloat16
        )
    spread(held, flat, 112, 36, 48)
    for k in range(3):
        payload[:, 1152 + 128 * k : 1280 + 128 * k] = flat[
            pl.ds(3 * core + k, 48, stride=6), :
        ].astype(jnp.bfloat16)
    spread(held, flat, 160, 216, 224)
    for k in range(36):
        ada[:, 128 * k : 128 * k + 128] = flat[pl.ds(k, 48, stride=36), :].astype(jnp.bfloat16)
    bias[...] = held[:, 384:400, :].astype(jnp.float32)
    relayout_two(held, payload_two, flat, core)


def relayout_two(held, payload, flat, core):
    spread(held, flat, 400, 144, 144)
    for k in range(12):
        payload[:, 128 * k : 128 * k + 128] = flat[
            pl.ds(12 * core + k, 48, stride=24), :
        ].astype(jnp.bfloat16)
    spread(held, flat, 544, 144, 144)
    for q in range(4):
        for k in range(3):
            lane = 1536 + 384 * q + 128 * k
            payload[:, lane : lane + 128] = flat[
                pl.ds(288 * q + 3 * core + k, 48, stride=6), :
            ].astype(jnp.bfloat16)


def pack_kernel(*refs):
    out, rows = refs[-2:]
    for j in range(6):
        for s in range(2):
            rows[6 * s + j : 6 * s + j + 1, :] = refs[j][s : s + 1, :]
    start = 12
    for ref in refs[6:10]:
        rows[start : start + ref.shape[0], :] = ref[...]
        start += ref.shape[0]
    rows[start:, :] = jnp.zeros((24 - start, D), jnp.float32)
    out[...] = rows[...].astype(jnp.bfloat16)


ANYWHERE = pl.BlockSpec(memory_space=pl.ANY)
SCALARS = pl.BlockSpec(memory_space=pltpu.SMEM)
LIMIT = pltpu.CompilerParams(vmem_limit_bytes=56 * 1024 * 1024)


VMEM = pl.BlockSpec(memory_space=pltpu.VMEM)


def relayout(kernel, rows, flat_rows, outs, where, mine, theirs):
    return pl.pallas_call(
        kernel,
        out_shape=outs,
        in_specs=[SCALARS, ANYWHERE, ANYWHERE],
        out_specs=[VMEM] * 4,
        scratch_shapes=[
            pltpu.VMEM((8, rows, 128), jnp.bfloat16),
            pltpu.VMEM((flat_rows, 128), jnp.float32),
            pltpu.SemaphoreType.DMA((2, 4)),
        ],
        compiler_params=LIMIT,
    )(where, mine, theirs)


def sources(groups):
    return [(group, k) for group, count in zip(groups, (4, 4, 4, 2, 2)) for k in range(count)]


def place_weights(spots, groups, qkv, proj, sems):
    copies = []
    for side in range(2):
        core = spots[32 + side]
        for i, (group, k) in enumerate(sources(groups[5 * side : 5 * side + 5])):
            rows = pl.ds(pl.multiple_of(48 * spots[16 * side + i], 16), 48)
            copies.append(
                pltpu.make_async_copy(
                    group.at[k, :, 0:1152],
                    qkv.at[rows, pl.ds(pl.multiple_of(1152 * core, 128), 1152)],
                    sems.at[side, i, 0],
                )
            )
            copies.append(
                pltpu.make_async_copy(
                    group.at[k, :, 1152:1536],
                    proj.at[rows, pl.ds(pl.multiple_of(384 * core, 128), 384)],
                    sems.at[side, i, 1],
                )
            )
    return copies


def dot(left, right, contract=(1, 0)):
    return lax.dot_general(
        left,
        right,
        (((contract[0],), (contract[1],)), ((), ())),
        preferred_element_type=jnp.float32,
    )


def low(values):
    return values.astype(jnp.bfloat16)


def normalize(values):
    centered = values - jnp.mean(values, axis=-1, keepdims=True)
    inverse = lax.rsqrt(jnp.mean(centered * centered, axis=-1, keepdims=True) + EPSILON)
    return centered * inverse, inverse


def norm_back(grad, normed, inverse):
    return inverse * (
        grad
        - jnp.mean(grad, axis=-1, keepdims=True)
        - normed * jnp.mean(grad * normed, axis=-1, keepdims=True)
    )


def part(modulation, s, j):
    return modulation[s : s + 1, D * j : D * j + D]


def lane_halves():
    lane = lax.broadcasted_iota(jnp.int32, (TOK, 128), 1)
    return lane < 64, lane >= 64


def probabilities(query, key):
    scores = dot(query, key, (1, 1)) * SCALE
    weights = jnp.exp(scores - jnp.max(scores, axis=-1, keepdims=True))
    return weights * (1.0 / jnp.sum(weights, axis=-1, keepdims=True))


def attention_kernel(spots, x, modulation, qkv_bias, proj_bias, *refs):
    groups, (h1, packed, mixed, attended, middle, h2, qkv, proj, sems) = refs[:10], refs[10:]
    copies = place_weights(spots, groups, qkv, proj, sems)
    for copy in copies:
        copy.start()
    for s in range(2):
        rows = slice(TOK * s, TOK * s + TOK)
        normed, _ = normalize(wide(x[rows]))
        h1[rows] = low(normed * (1.0 + part(modulation, s, 1)) + part(modulation, s, 0))
    for copy in copies:
        copy.wait()
    first_half, _ = lane_halves()
    zero = jnp.zeros((TOK, 128), jnp.bfloat16)
    for s in range(2):
        rows = slice(TOK * s, TOK * s + TOK)
        for t in range(3):
            lanes = slice(D * t, D * t + D)
            packed[rows, lanes] = low(dot(h1[rows], qkv[:, lanes]) + qkv_bias[:, lanes])
        for pair in range(6):
            query = packed[rows, 128 * pair : 128 * pair + 128]
            key = packed[rows, D + 128 * pair : D + 128 * pair + 128]
            value = packed[rows, 2 * D + 128 * pair : 2 * D + 128 * pair + 128]
            one = dot(low(probabilities(jnp.where(first_half, query, zero), key)), value)
            two = dot(low(probabilities(jnp.where(first_half, zero, query), key)), value)
            mixed[rows, 128 * pair : 128 * pair + 128] = low(jnp.where(first_half, one, two))
        branch = dot(mixed[rows], proj[...]) + proj_bias[...]
        attended[rows] = branch
        after = wide(x[rows]) + part(modulation, s, 2) * branch
        middle[rows] = after
        normed, _ = normalize(after)
        h2[rows] = low(normed * (1.0 + part(modulation, s, 4)) + part(modulation, s, 3))


def total(values):
    return jnp.sum(values, axis=0, keepdims=True)


def place_mlp(where, mine, theirs, up, down, sems):
    copies = []
    for side, source in enumerate((mine, theirs)):
        core = where[1] if side == 0 else 1 - where[1]
        copies.append(
            pltpu.make_async_copy(
                source.at[:, 0:1536],
                up.at[:, pl.ds(pl.multiple_of(1536 * core, 128), 1536)],
                sems.at[side, 64],
            )
        )
        lanes = pl.ds(pl.multiple_of(384 * core, 128), 384)
        for b in range(16):
            for q in range(4):
                start = 192 * b + 48 * q
                copies.append(
                    pltpu.make_async_copy(
                        source.at[48 * b : 48 * b + 48, 1536 + 384 * q : 1920 + 384 * q],
                        down.at[start : start + 48, lanes],
                        sems.at[side, 4 * b + q],
                    )
                )
    return copies


def mlp_kernel(
    where, middle, attended, h2, mixed, cotangent, modulation, up_bias, down_bias, mine, theirs,
    result, middle_grad, branch_grad, summand,
    gate_one, shift_two, scale_two, gate_two, proj_sum, down_sum, up_sum,
    up, down, active, hidden_grad, out_grad, branch, hidden_two, sems,
):
    copies = place_mlp(where, mine, theirs, up, down, sems)
    for copy in copies:
        copy.start()
    for s in range(2):
        rows = slice(TOK * s, TOK * s + TOK)
        out_grad[rows] = low(part(modulation, s, 5) * wide(cotangent[rows]))
    for copy in copies:
        copy.wait()
    for s in range(2):
        rows = slice(TOK * s, TOK * s + TOK)
        for t in range(6):
            lanes = slice(512 * t, 512 * t + 512)
            value = dot(h2[rows], up[:, lanes]) + up_bias[:, lanes]
            square = value * value
            bend = jnp.tanh(GELU * (value + 0.044715 * (square * value)))
            active[rows, lanes] = low(0.5 * value * (1.0 + bend))
            slope = 0.5 * (1.0 + bend) + 0.5 * value * (1.0 - bend * bend) * (
                GELU * (1.0 + 3 * 0.044715 * square)
            )
            grad = low(dot(out_grad[rows], down[lanes, :], (1, 1)) * slope)
            hidden_grad[rows, lanes] = grad
            sums = total(wide(grad))
            if s == 0:
                up_sum[:, lanes] = sums
            else:
                up_sum[:, lanes] = up_sum[:, lanes] + sums
        branch[...] = dot(active[rows], down[...]) + down_bias[...]
        hidden_two[...] = dot(hidden_grad[rows], up[...], (1, 1))
        given = wide(cotangent[rows])
        after = middle[rows]
        result[rows] = low(after + part(modulation, s, 5) * branch[...])
        gate_two[s : s + 1] = total(given * branch[...])
        normed, inverse = normalize(after)
        grad = hidden_two[...]
        shift_two[s : s + 1] = total(grad)
        scale_two[s : s + 1] = total(grad * normed)
        grad = given + norm_back(grad * (1.0 + part(modulation, s, 4)), normed, inverse)
        middle_grad[rows] = grad
        gate_one[s : s + 1] = total(grad * attended[rows])
        branch_grad[rows] = low(part(modulation, s, 2) * grad)
    proj_sum[...] = total(wide(branch_grad[...]))
    down_sum[...] = total(wide(out_grad[...]))
    for t in range(4):
        lanes = slice(D * t, D * t + D)
        summand[:, lanes] = low(dot(h2[...], hidden_grad[:, lanes], (0, 0)))
    for t in range(8):
        tile = low(dot(active[:, 384 * t : 384 * t + 384], out_grad[...], (0, 0)))
        for j in range(8):
            b, q = 2 * t + j // 4, j % 4
            summand[48 * b : 48 * b + 48, FF + D * q : FF + D * q + D] = tile[
                48 * j : 48 * j + 48
            ]
    summand[:, 2 * FF :] = low(dot(mixed[...], branch_grad[...], (0, 0)))


def attention_back_kernel(
    where, x, modulation, packed, h1, branch_grad, middle_grad, qkv, proj,
    tokens_grad, mine, theirs, shift_one, scale_one, qv_sum,
    mixed_grad, packed_grad,
):
    first_half, _ = lane_halves()
    zero = jnp.zeros((TOK, 128), jnp.bfloat16)
    for s in range(2):
        rows = slice(TOK * s, TOK * s + TOK)
        mixed_grad[...] = low(dot(branch_grad[rows], proj[...], (1, 1)))
        for pair in range(6):
            lanes = slice(128 * pair, 128 * pair + 128)
            query = packed[rows, lanes]
            key = packed[rows, D + 128 * pair : D + 128 * pair + 128]
            value = packed[rows, 2 * D + 128 * pair : 2 * D + 128 * pair + 128]
            grad = mixed_grad[:, lanes]
            query_grads = []
            key_grad = None
            for half in range(2):
                if half == 0:
                    own_query = jnp.where(first_half, query, zero)
                    own_grad = jnp.where(first_half, grad, zero)
                else:
                    own_query = jnp.where(first_half, zero, query)
                    own_grad = jnp.where(first_half, zero, grad)
                probs = probabilities(own_query, key)
                from_value = dot(low(probs), own_grad, (0, 0))
                probs_grad = dot(own_grad, value, (1, 1))
                scores_grad = low(
                    probs
                    * (probs_grad - jnp.sum(probs_grad * probs, axis=-1, keepdims=True))
                )
                query_grads.append(dot(scores_grad, key))
                from_key = dot(scores_grad, own_query, (0, 0))
                if key_grad is None:
                    key_grad, value_grad = from_key, from_value
                else:
                    key_grad, value_grad = key_grad + from_key, value_grad + from_value
            packed_grad[rows, lanes] = low(
                jnp.where(first_half, query_grads[0], query_grads[1]) * SCALE
            )
            packed_grad[rows, D + 128 * pair : D + 128 * pair + 128] = low(key_grad * SCALE)
            packed_grad[rows, 2 * D + 128 * pair : 2 * D + 128 * pair + 128] = low(value_grad)
        grad = dot(packed_grad[rows], qkv[...], (1, 1))
        normed, inverse = normalize(wide(x[rows]))
        shift_one[s : s + 1] = total(grad)
        scale_one[s : s + 1] = total(grad * normed)
        tokens_grad[rows] = low(
            middle_grad[rows] + norm_back(grad * (1.0 + part(modulation, s, 1)), normed, inverse)
        )
    qv_sum[0:1] = total(wide(packed_grad[:, 0:D]))
    qv_sum[1:2] = total(wide(packed_grad[:, 2 * D :]))
    for out, core in ((theirs, 1 - where[1]), (mine, where[1])):
        for t in range(3):
            lanes = pl.ds(pl.multiple_of(1152 * core + 384 * t, 128), 384)
            out[:, 384 * t : 384 * t + 384] = low(dot(h1[...], packed_grad[:, lanes], (0, 0)))


def shaped(*shape, dtype=jnp.float32):
    return jax.ShapeDtypeStruct(shape, dtype)


def cost(flops, moved):
    return pl.CostEstimate(flops=flops, bytes_accessed=moved, transcendentals=0)


def sum_kernel(spots, mine, received, out):
    for i in range(16):
        rows = pl.ds(pl.multiple_of(48 * spots[i], 16), 48)
        out[i] = low(wide(mine[rows, :]) + wide(received[rows, :]))


def wide(values):
    return values.astype(jnp.float32)


def ring_sum(blocks):
    far, high, low_, base = blocks[0:4], blocks[4:8], blocks[8:12], blocks[12:16]
    far_low = send(far[:2], "second", 1)
    far_high = send(far[2:], "second", -1)
    high = jnp.concatenate([(wide(high[:2]) + wide(far_low)).astype(jnp.bfloat16), high[2:]])
    low_ = jnp.concatenate([low_[:2], (wide(low_[2:]) + wide(far_high)).astype(jnp.bfloat16)])
    from_low = send(high, "second", 1)
    from_high = send(low_, "second", -1)
    base = wide(base) + wide(from_low) + wide(from_high)
    total = base[0]
    for k in (1, 2, 3):
        total = total + wide(send(base[k].astype(jnp.bfloat16), "first", k))
    return total


def column_sum(rows, z):
    parts = rows.reshape(4, 12, -1)
    parts = lax.dynamic_slice_in_dim(jnp.concatenate([parts, parts]), z, 4, axis=0)
    total = parts[0]
    for k in (1, 2, 3):
        total = total + wide(send(parts[k].astype(jnp.bfloat16), "z", k))
    return total.reshape(2, 6, -1)


def other_half(values, core):
    half = values.shape[-1] // 2
    return jnp.where(core == 0, values[:, half:], values[:, :half])


def own_half(values, core):
    half = values.shape[-1] // 2
    return jnp.where(core == 0, values[:, :half], values[:, half:])


def joined(mine, received, core):
    return jnp.where(
        core == 0,
        jnp.concatenate([mine, received], axis=-1),
        jnp.concatenate([received, mine], axis=-1),
    ).reshape(-1)


def body(
    tokens,
    condition,
    cotangent,
    ada_weight,
    ada_bias,
    qkv_weight,
    qv_bias,
    proj_weight,
    proj_bias,
    fc1_weight,
    fc1_bias,
    fc2_weight,
    fc2_bias,
):
    table = lax.dynamic_index_in_dim(
        jnp.asarray(TABLE), lax.axis_index(AXES), axis=0, keepdims=False
    )
    core, z, plane_index = table[0], table[1], table[2]
    where = table[3:5]
    spots = table[8:42]
    sum_spots = table[48:65]
    reverse_spots = table[72:88]
    order = table[88:104]
    def padded(values, rows):
        values = values.reshape(-1, 128)
        return jnp.concatenate([values, jnp.zeros((rows - values.shape[0], 128), jnp.bfloat16)])

    bias_row = jnp.zeros((128,), jnp.bfloat16)
    start = 0
    for bias in (qv_bias, proj_bias, fc1_bias, fc2_bias, ada_bias):
        stop = start + bias.shape[0]
        bias_row = bias_row + jnp.pad(bias, (start, 128 - stop))
        start = stop
    own_one = jnp.concatenate(
        [
            padded(qkv_weight, 112),
            padded(proj_weight, 48),
            padded(ada_weight, 224),
            padded(bias_row, 16),
            fc1_weight.reshape(-1, 128),
            fc2_weight.reshape(-1, 128),
        ]
    )
    column_one = gathered(own_one, "z")
    plane_small = gathered(gathered(padded(condition, 16), "first"), "second").reshape(16, 16, 128)
    column_one_in = send(column_one, "core")
    payload_one, ada_rows, bias_block, payload_two = relayout(
        relayout_one_kernel,
        ROWS_ONE,
        1728,
        [
            jax.ShapeDtypeStruct((48, 1536), jnp.bfloat16),
            jax.ShapeDtypeStruct((48, 6 * D), jnp.bfloat16),
            jax.ShapeDtypeStruct((8, 16, 128), jnp.float32),
            jax.ShapeDtypeStruct((48, FF), jnp.bfloat16),
        ],
        where,
        column_one,
        column_one_in,
    )
    weights_two = lax.all_gather(payload_two, PLANE, axis=0, tiled=True)
    embed_plane = plane_small[:, :12].reshape(32, D)
    embed_plane_low = jax.nn.silu(embed_plane.astype(jnp.float32)).astype(jnp.bfloat16)
    embed_rows = lax.dynamic_slice(embed_plane_low, (0, 48 * plane_index), (32, 48))
    bias_block = bias_block[:, 0, :]
    ada_bias_row = lax.dynamic_update_slice(
        jnp.zeros((6 * D,), jnp.float32), bias_block[:, 48:84].reshape(-1), (288 * plane_index,)
    )
    bias_slots = lax.dynamic_update_slice(
        jnp.zeros((16, 384), jnp.float32),
        bias_block[:, 0:48].reshape(1, 384),
        (plane_index, 0),
    )
    modulation_part = jnp.concatenate(
        [
            jnp.dot(embed_rows, ada_rows, preferred_element_type=jnp.float32) + ada_bias_row,
            jnp.broadcast_to(bias_slots.reshape(1, 2, 4 * D), (16, 2, 4 * D)).reshape(32, 4 * D),
        ],
        axis=1,
    ).reshape(4, 8, 10 * D)
    base = gathered(payload_one, "first")
    rows_in = [send(modulation_part[k], "second", -k) for k in (1, 2, 3)]
    base, rows_in = lax.optimization_barrier((base, rows_in))
    modulation_rows = (modulation_part[0] + rows_in[0] + rows_in[1] + rows_in[2]).reshape(
        4, 2, 10 * D
    )
    under = send(base, "second", 1)
    over = send(base, "second", -1)
    modulation = modulation_rows[0]
    for k in (1, 2, 3):
        modulation = modulation + send(modulation_rows[k], "first", -k)
    far_under = send(under[:2], "second", 1)
    far_over = send(over[2:], "second", -1)
    mine_one = [base, under, over, far_under, far_over]
    theirs_one = [send(group, "core") for group in mine_one]
    bias_rows = modulation[:, 6 * D :].reshape(16, 8, 48)
    modulation = modulation[:, : 6 * D]
    qv_vec = bias_rows[:, :, 0:12].reshape(-1)
    projection_bias = bias_rows[:, :, 12:18].reshape(-1)
    up_projection_bias = bias_rows[:, :, 18:42].reshape(-1)
    down_vec = bias_rows[:, :, 42:48].reshape(-1)
    modulation, theirs_one, weights_two = lax.optimization_barrier(
        (modulation, theirs_one, weights_two)
    )
    weights_two_in = send(weights_two, "core")
    bias_full = jnp.concatenate([qv_vec[:D], jnp.zeros((D,), jnp.float32), qv_vec[D:]])
    latents = tokens.reshape(2 * TOK, D)
    h1, packed, mixed, attended, middle, h2, qkv_whole, proj_whole = pl.pallas_call(
        attention_kernel,
        out_shape=[
            shaped(512, D, dtype=jnp.bfloat16),
            shaped(512, 3 * D, dtype=jnp.bfloat16),
            shaped(512, D, dtype=jnp.bfloat16),
            shaped(512, D),
            shaped(512, D),
            shaped(512, D, dtype=jnp.bfloat16),
            shaped(D, 3 * D, dtype=jnp.bfloat16),
            shaped(D, D, dtype=jnp.bfloat16),
        ],
        in_specs=[SCALARS] + [VMEM] * 4 + [ANYWHERE] * 10,
        out_specs=[VMEM] * 8,
        scratch_shapes=[pltpu.SemaphoreType.DMA((2, 16, 2))],
        compiler_params=LIMIT,
        cost_estimate=cost(3 * 10**9, 2 * 10**7),
    )(
        spots,
        latents,
        modulation,
        bias_full.reshape(1, 3 * D),
        projection_bias.reshape(1, D),
        *mine_one,
        *theirs_one,
    )
    (
        result,
        middle_grad,
        branch_grad,
        summand_two,
        gate_attn_grad,
        shift_mlp_grad,
        scale_mlp_grad,
        gate_mlp_grad,
        proj_bias_grad,
        down_bias_grad,
        up_bias_grad,
    ) = pl.pallas_call(
        mlp_kernel,
        out_shape=[
            shaped(512, D, dtype=jnp.bfloat16),
            shaped(512, D),
            shaped(512, D, dtype=jnp.bfloat16),
            shaped(D, 9 * D, dtype=jnp.bfloat16),
            shaped(2, D),
            shaped(2, D),
            shaped(2, D),
            shaped(2, D),
            shaped(1, D),
            shaped(1, D),
            shaped(1, FF),
        ],
        in_specs=[SCALARS] + [VMEM] * 8 + [ANYWHERE] * 2,
        out_specs=[VMEM] * 11,
        scratch_shapes=[
            pltpu.VMEM((D, FF), jnp.bfloat16),
            pltpu.VMEM((FF, D), jnp.bfloat16),
            pltpu.VMEM((512, FF), jnp.bfloat16),
            pltpu.VMEM((512, FF), jnp.bfloat16),
            pltpu.VMEM((512, D), jnp.bfloat16),
            pltpu.VMEM((TOK, D), jnp.float32),
            pltpu.VMEM((TOK, D), jnp.float32),
            pltpu.SemaphoreType.DMA((2, 65)),
        ],
        compiler_params=LIMIT,
        cost_estimate=cost(15 * 10**9, 3 * 10**7),
    )(
        where,
        middle,
        attended,
        h2,
        mixed,
        cotangent.reshape(2 * TOK, D),
        modulation,
        up_projection_bias.reshape(1, FF),
        down_vec.reshape(1, D),
        weights_two,
        weights_two_in,
    )
    branch_grad, summand_two = lax.optimization_barrier((branch_grad, summand_two))
    rows_two = wide(lax.psum_scatter(summand_two, PLANE, scatter_dimension=0, tiled=True))
    input_grad, grad_mine, grad_theirs, shift_attn_grad, scale_attn_grad, qv_bias_grad = (
        pl.pallas_call(
            attention_back_kernel,
            out_shape=[
                shaped(512, D, dtype=jnp.bfloat16),
                shaped(D, 1152, dtype=jnp.bfloat16),
                shaped(D, 1152, dtype=jnp.bfloat16),
                shaped(2, D),
                shaped(2, D),
                shaped(2, D),
            ],
            in_specs=[SCALARS] + [VMEM] * 8,
            out_specs=[VMEM] * 6,
            scratch_shapes=[
                pltpu.VMEM((TOK, D), jnp.bfloat16),
                pltpu.VMEM((512, 3 * D), jnp.bfloat16),
            ],
            compiler_params=LIMIT,
            cost_estimate=cost(8 * 10**9, 2 * 10**7),
        )(where, latents, modulation, packed, h1, branch_grad, middle_grad, qkv_whole, proj_whole)
    )
    packed_small = pl.pallas_call(
        pack_kernel,
        out_shape=jax.ShapeDtypeStruct((24, D), jnp.bfloat16),
        in_specs=[VMEM] * 10,
        out_specs=VMEM,
        scratch_shapes=[pltpu.VMEM((24, D), jnp.float32)],
    )(
        shift_attn_grad,
        scale_attn_grad,
        gate_attn_grad,
        shift_mlp_grad,
        scale_mlp_grad,
        gate_mlp_grad,
        qv_bias_grad,
        proj_bias_grad,
        up_bias_grad.reshape(4, D),
        down_bias_grad,
    )
    plane_grads = gathered(gathered(packed_small, "first"), "second").reshape(16, 24, D)
    modulation_grads = plane_grads[:, :12].reshape(32, 6 * D)
    bias_sums = jnp.sum(plane_grads[:, 12:20], axis=0, dtype=jnp.float32).reshape(-1)
    ada_grad = jnp.einsum(
        "sd,se->de", embed_rows, modulation_grads, preferred_element_type=jnp.float32
    )
    ada_bias_sums = jnp.sum(modulation_grads, axis=0, dtype=jnp.float32)
    embed_part = jnp.einsum(
        "se,de->sd", modulation_grads, ada_rows, preferred_element_type=jnp.float32
    ).reshape(4, 8, 48)
    embed_rows_in = jnp.stack(
        [embed_part[0]] + [send(embed_part[k], "second", -k) for k in (1, 2, 3)]
    ).reshape(4, 4, 2, 48)
    embed_parts = jnp.stack(
        [embed_rows_in[:, 0]] + [send(embed_rows_in[:, k], "first", -k) for k in (1, 2, 3)],
        axis=1,
    ).reshape(16, 2, 48)
    embed_sum = jnp.take(embed_parts, order, axis=0).transpose(1, 0, 2).reshape(2, D)
    _, silu_back = jax.vjp(jax.nn.silu, condition.astype(jnp.float32))
    embed_grad = silu_back(embed_sum)[0]

    blocks_one = pl.pallas_call(
        sum_kernel,
        out_shape=shaped(16, 48, 1152, dtype=jnp.bfloat16),
        in_specs=[SCALARS, VMEM, VMEM],
        out_specs=VMEM,
        compiler_params=LIMIT,
    )(sum_spots, grad_mine, send(grad_theirs, "core"))
    rows_one = ring_sum(blocks_one)
    bias_parts = []
    start = 0
    for size in (12, 6, 24, 6):
        bias_parts.append(
            lax.dynamic_slice(
                bias_sums[start : start + 128 * size], (8 * size * plane_index,), (8 * size,)
            ).reshape(8, size)
        )
        start += 128 * size
    bias_parts.append(
        lax.dynamic_slice(ada_bias_sums, (288 * plane_index,), (288,)).reshape(8, 36)
    )
    bias_block = jnp.pad(
        jnp.concatenate(bias_parts, axis=1).reshape(48, 14), ((0, 0), (0, 128 - 14))
    )
    down_rows = rows_two[:, FF : 2 * FF].reshape(48, 4, D).transpose(1, 0, 2).reshape(48, FF)
    wide_rows = jnp.concatenate(
        [ada_grad, rows_two[:, :FF], down_rows, rows_two[:, 2 * FF :]], axis=-1
    )
    pieces = []
    start = 0
    for width in (6 * D, FF, D, D, D, D, D):
        pieces.append(wide_rows[:, start : start + width])
        start += width
    out_half = jnp.concatenate([other_half(piece, core) for piece in pieces] + [bias_block], axis=-1)
    own = jnp.concatenate([own_half(piece, core) for piece in pieces] + [bias_block], axis=-1)
    own = own + wide(send(out_half.astype(jnp.bfloat16), "core"))
    rows_all = column_sum(jnp.concatenate([rows_one, own], axis=-1), z)
    mine = jnp.where(core == 0, rows_all[0], rows_all[1])
    received = wide(
        send(
            jnp.where(core == 0, rows_all[1], rows_all[0])[:, :6912].astype(jnp.bfloat16),
            "core",
        )
    )

    def cut(start, width, groups=1):
        return joined(
            mine[:, start : start + width].reshape(6, groups, -1),
            received[:, start : start + width].reshape(6, groups, -1),
            core,
        )

    bias_shard = mine[:, 6912:6926].reshape(-1)
    return (
        result.reshape(tokens.shape),
        input_grad.reshape(tokens.shape),
        embed_grad.astype(jnp.bfloat16),
        cut(1152, 2304),
        bias_shard[48:84],
        cut(0, 1152),
        bias_shard[0:12],
        cut(6528, 384),
        bias_shard[12:18],
        cut(3456, 1536),
        bias_shard[18:42],
        cut(4992, 1536, 4),
        bias_shard[42:48],
    )


def solution(mesh):
    return jax.shard_map(
        body,
        mesh=Mesh(mesh.devices.reshape(4, 4, 4, 2), AXES),
        in_specs=(
            P(AXES, None, None),
            P(AXES, None),
            P(AXES, None, None),
            P(AXES),
            P(AXES),
            P(AXES),
            P(AXES),
            P(AXES),
            P(AXES),
            P(AXES),
            P(AXES),
            P(AXES),
            P(AXES),
        ),
        out_specs=(
            P(AXES, None, None),
            P(AXES, None, None),
            P(AXES, None),
            P(AXES),
            P(AXES),
            P(AXES),
            P(AXES),
            P(AXES),
            P(AXES),
            P(AXES),
            P(AXES),
            P(AXES),
            P(AXES),
        ),
        check_vma=False,
    )
```
